32 devices in a mesh: dp: 4 (over y, x), expert: 8 (over z, core).
Axes of the slice: x: 2, y: 2, z: 4, core: 2. Of those that a mesh axis runs over, the one named last changes fastest.
Arguments:
- tokens: bfloat16 [4096, 768], P(('dp', 'expert')), may hold values from -6 to 6
- w_query: bfloat16 [768, 768], P('dp'), may hold values from -0.109375 to 0.109375
- w_key: bfloat16 [768, 768], P('dp'), may hold values from -0.109375 to 0.109375
- w_value: bfloat16 [768, 768], P('dp'), may hold values from -0.21875 to 0.21875
- w_attn_out: bfloat16 [768, 768], P('dp'), may hold values from -0.875 to 0.875
- w_router: bfloat16 [768, 8], P('dp'), may hold values from -0.109375 to 0.109375
- norm1_gain: bfloat16 [768], P('dp'), may hold values from 0.5 to 1.5
- norm2_gain: bfloat16 [768], P('dp'), may hold values from 0.5 to 1.5
- bias_table: bfloat16 [32, 12], P('dp'), may hold values from -4 to 4
- w_expert_in: bfloat16 [8, 768, 3072], P('expert', None, 'dp'), may hold values from -0.21875 to 0.21875
- w_expert_out: bfloat16 [8, 3072, 768], P('expert', 'dp'), may hold values from -1.25 to 1.25
- routes: int32 [4096, 1], P(('dp', 'expert')), may hold values from 0 to 7; in each aligned block of 128 rows (0 to 127, 128 to 255, ...) at most 20 rows name the same one
- segments: int32 [4096], P(('dp', 'expert')), may hold values from 0 to 31, as said below
- cotangent: bfloat16 [4096, 768], P(('dp', 'expert')), may hold values from -6 to 6
Outputs:
- layer_out: bfloat16 [4096, 768], P(('dp', 'expert'))
- d_tokens: float32 [4096, 768], P(('dp', 'expert'))
- grad_query: float32 [768, 768], P('dp')
- grad_key: float32 [768, 768], P('dp')
- grad_value: float32 [768, 768], P('dp')
- grad_attn_out: float32 [768, 768], P('dp')
- grad_router: float32 [768, 8], P('dp')
- grad_norm1_gain: float32 [768], P('dp')
- grad_norm2_gain: float32 [768], P('dp')
- grad_bias_table: float32 [32, 12], P('dp')
- grad_expert_in: float32 [8, 768, 3072], P('expert', None, 'dp')
- grad_expert_out: float32 [8, 3072, 768], P('expert', 'dp')
The draws below stay inside these ranges and needn't reach their ends.
Inputs may be any that keep to these rules, and one draw needn't show every extreme that they name: `routes`: within the 128 rows of one device no expert is named more than 20 times, and in every draw some expert of some device is named exactly 20 times. `segments`: within one device the values never fall along the rows and the first row holds 0; the largest value is reached on some device in every draw.
All inputs are finite; a program needn't handle non-finite values.
Results may differ from the reference program's by a relative error of at most 0.022.
Values may be sent and summed in bfloat16 or wider, within the bound.
No kernel may reach another device: no remote copies, remote signals or barrier semaphores. Data moves between devices by JAX's collectives and lax.ppermute only.
A program may use at most 128 MiB of HBM per device.

```python
import math
import jax
import jax.numpy as jnp
import numpy as np
from jax import lax

D = 768
HEADS = 12
HEAD = 64
FF = 3072
BUCKETS = 32
TOK_DEV = 128
EXPERTS = 8
CAP = 20
TOKENS = 4096


def draw_segments(key, part):
    key = jax.random.fold_in(key, 7)
    spread_key, start_key = jax.random.split(key)
    blocks = TOKENS // TOK_DEV
    spacing = jax.random.randint(spread_key, (blocks, 1), 4, 2 * TOK_DEV)
    raw_bits = jax.random.randint(start_key, (blocks, TOK_DEV), 0, 1048576)
    places = jnp.arange(TOK_DEV, dtype=jnp.int32)[None, :]
    block_ids = jnp.arange(blocks, dtype=jnp.int32)[:, None]
    starts = jnp.where(places == 0, 1, jnp.where(raw_bits % spacing == 0, 1, 0))
    starts = jnp.where(block_ids == 0, jnp.where(places == 0, 1, 0), starts)
    starts = jnp.where(block_ids == 1, jnp.where(places % 4 == 0, 1, 0), starts)
    numbers = jnp.minimum(jnp.cumsum(starts, axis=1) - 1, TOK_DEV // 4 - 1)
    return numbers.astype(jnp.int32).reshape(TOKENS)


def block_scale(stream_key, extent, shards, low, high):
    def one(dim, shards_of):
        draws = jax.random.uniform(jax.random.fold_in(jax.random.fold_in(stream_key, 6), dim), (shards_of,), jnp.float32, low / len(shards), high / len(shards))
        return jnp.repeat(jnp.exp(draws), extent[dim] // shards_of).reshape((-1,) + (1,) * (len(extent) - dim - 1))

    level = one(*shards[0])
    for cut in shards[1:]:
        level = level * one(*cut)
    return level


def assign_block(rng, own, number, rows, amount, top, limit, skew):
    sequence = jax.random.permutation(rng, amount)
    packed, usual = shares(amount, rows * top, limit, skew, True), shares(amount, rows * top, limit, skew, False)
    places = jnp.arange(amount)

    def named(tallies, turn):
        used = int((tallies > 0).sum())
        fixed = max(1, used // 4)
        passed = fixed + (places - fixed + turn * (used - fixed)) % max(1, amount - fixed)
        return jnp.zeros((amount,), jnp.int32).at[sequence[jnp.where(places < fixed, places, passed)]].set(jnp.asarray(tallies, jnp.int32))

    tallies = jnp.where(number % 4 == 0, named(packed, number // 4), named(usual, number - number // 4 - 1))
    mixed = jax.random.permutation(jax.random.fold_in(own, 3), amount)
    donor, receiver = mixed[0:amount // 2 * 2:2], mixed[1:amount // 2 * 2:2]
    room = jnp.minimum(tallies[donor] - 1, limit - tallies[receiver]) // 2
    room = jnp.where((donor == sequence[0]) | (receiver == sequence[0]) | (tallies[receiver] == 0), 0, jnp.maximum(room, 0))
    passed = jax.random.randint(jax.random.fold_in(own, 4), (amount // 2,), 0, 1 << 20) % (room + 1)
    tallies = tallies.at[donor].add(-passed).at[receiver].add(passed)
    items = jnp.searchsorted(jnp.cumsum(tallies), jnp.arange(rows * top), side="right").astype(jnp.int32)
    table = items.reshape(top, rows).T
    table = table[jax.random.permutation(jax.random.fold_in(own, 1), rows)]
    turn = jax.random.randint(jax.random.fold_in(own, 2), (rows, 1), 0, top)
    return jnp.take_along_axis(table, (jnp.arange(top)[None, :] + turn) % top, axis=1)


def shares(amount, total, most, slope, full):
    weights = [(1 << 20) // math.isqrt(rank ** slope) + 1 for rank in range(1, amount + 1)]
    largest = most if full else min(most, max(-(-total // amount), total * weights[0] // sum(weights)))
    least = 1 if total - largest >= amount - 1 else 0
    holding, surplus = [largest] + [least] * (amount - 1), total - largest - least * (amount - 1)
    while surplus > 0:
        movable = [i for i in range(1, amount) if holding[i] < largest] or [i for i in range(1, amount) if holding[i] < most]
        mass, left = sum([weights[i] for i in movable]), surplus
        for i in movable:
            more = min(most - holding[i], max(1, left * weights[i] // mass), surplus)
            holding[i] = holding[i] + more
            surplus = surplus - more
    return np.array(holding)


def centred(rng, shape, scale, reach, cuts=(), held_as=jnp.bfloat16):
    values = jax.random.normal(rng, shape, jnp.float32) * scale
    if len(cuts) > 0:
        values = block_scale(rng, shape, cuts, -0.22, 0.18) * values
    return jnp.clip(values, min=-reach, max=reach).astype(held_as)


def setup_inputs(seed: int = 0) -> dict:
    key_list = jax.random.split(jax.random.key(seed), 15)
    tokens = centred(key_list[0], (TOKENS, D), 1.0, 6.0, ((0, 32),))
    w_query = centred(key_list[1], (D, D), (4 * D) ** -0.5, 0.109375, ((0, 4),))
    w_key = centred(key_list[2], (D, D), (4 * D) ** -0.5, 0.109375, ((0, 4),))
    w_value = centred(key_list[3], (D, D), D ** -0.5, 0.21875, ((0, 4),))
    w_attn_out = centred(key_list[4], (D, D), (D // 16) ** -0.5, 0.875, ((0, 4),))
    w_router = centred(key_list[5], (D, EXPERTS), (4 * D) ** -0.5, 0.109375, ((0, 4),))
    norm1_gain = jnp.clip(1.0 + 0.1 * jax.random.normal(key_list[6], (D,), jnp.float32), 0.5, 1.5).astype(jnp.bfloat16)
    norm2_gain = jnp.clip(1.0 + 0.1 * jax.random.normal(key_list[7], (D,), jnp.float32), 0.5, 1.5).astype(jnp.bfloat16)
    bias_table = centred(key_list[8], (BUCKETS, HEADS), 1.0, 4.0, ((0, 4),))
    w_expert_in = centred(key_list[9], (EXPERTS, D, FF), D ** -0.5, 0.21875, ((0, 8), (2, 4)))
    w_expert_out = centred(key_list[10], (EXPERTS, FF, D), (max(1, FF // (2 * EXPERTS * EXPERTS))) ** -0.5, 1.25, ((0, 8), (1, 4)))
    routes_keys = jax.random.split(jax.random.fold_in(key_list[11], 1), TOKENS // TOK_DEV)
    routes_turns = jax.random.permutation(jax.random.fold_in(key_list[11], 3), TOKENS // TOK_DEV)
    routes = jax.vmap(lambda own, number: assign_block(jax.random.fold_in(key_list[11], 2), own, number, TOK_DEV, EXPERTS, 1, CAP, 1))(routes_keys, routes_turns).reshape((TOKENS, 1))
    segments = draw_segments(jax.random.fold_in(key_list[14], 71), 0)
    cotangent = centred(key_list[13], (TOKENS, D), 1.0, 6.0, ((0, 32),))
    return {"tokens": tokens, "w_query": w_query, "w_key": w_key, "w_value": w_value, "w_attn_out": w_attn_out, "w_router": w_router, "norm1_gain": norm1_gain, "norm2_gain": norm2_gain, "bias_table": bias_table, "w_expert_in": w_expert_in, "w_expert_out": w_expert_out, "routes": routes, "segments": segments, "cotangent": cotangent}


@jax.custom_vjp
def low(v):
    return lax.optimization_barrier(v.astype(jnp.bfloat16)).astype(jnp.float32)

@jax.custom_vjp
def low_back(v):
    return v

def low_keep(v):
    return (low(v), None)

def low_pass(kept, grad):
    return (grad,)

def back_keep(v):
    return (v, None)

def back_low(kept, grad):
    return (low(grad),)
low.defvjp(low_keep, low_pass)
low_back.defvjp(back_keep, back_low)
eps = 1e-06
bucket_edges = (12, 16, 23, 32, 46, 64, 91)

def bucket_ids(offsets):
    distance = -offsets
    upper_half = jnp.where(distance < 0, 16, 0).astype(jnp.int32)
    magnitude = jnp.abs(distance).astype(jnp.int32)
    far_bucket = jnp.full_like(magnitude, 8)
    for threshold in bucket_edges:
        far_bucket = far_bucket + (magnitude >= threshold).astype(jnp.int32)
    return (upper_half + jnp.where(magnitude < 8, magnitude, far_bucket)).astype(jnp.int32)

def relative_bias(table, length):
    offsets = jnp.arange(2 * length - 1, dtype=jnp.int32) - (length - 1)
    chosen = bucket_ids(offsets)
    onehot_rows = (chosen[:, None] == jnp.arange(table.shape[0], dtype=jnp.int32)[None, :]).astype(jnp.float32)
    per_offset = jnp.dot(onehot_rows, table, precision=lax.Precision.HIGHEST, preferred_element_type=jnp.float32)
    places = jnp.arange(length, dtype=jnp.int32)
    lookup = places[None, :] - places[:, None] + (length - 1)
    return jnp.transpose(per_offset[lookup], (2, 0, 1))

def highest(left, right):
    return jnp.dot(left, right, precision=lax.Precision.HIGHEST, preferred_element_type=jnp.float32)

def rounded_both(value):
    return low_back(low(value))

def rms_normed(value, gain_row):
    return value * lax.rsqrt(lax.optimization_barrier(jnp.mean(value * value, axis=-1, keepdims=True)) + eps) * gain_row

def attend_block(block_rows, block_docs, w_query, w_key, w_value, w_attn_out, norm1_gain, bias_table):
    length = block_rows.shape[0]
    normed = low(rms_normed(block_rows, norm1_gain))
    query_rows = rounded_both(highest(normed, w_query)).reshape(length, HEADS, HEAD)
    key_rows = rounded_both(highest(normed, w_key)).reshape(length, HEADS, HEAD)
    value_rows = rounded_both(highest(normed, w_value)).reshape(length, HEADS, HEAD)
    scores = jnp.einsum('thd,shd->hts', query_rows, key_rows, precision=lax.Precision.HIGHEST)
    scores = low_back(scores + relative_bias(bias_table, length))
    same_doc = block_docs[:, None] == block_docs[None, :]
    scores = jnp.where(same_doc[None], scores, -1000000000.0)
    weights = low(jax.nn.softmax(scores, axis=-1))
    context = jnp.einsum('hts,shd->thd', weights, value_rows, precision=lax.Precision.HIGHEST)
    context = rounded_both(context).reshape(length, D)
    return block_rows + low_back(highest(context, w_attn_out))

def expert_block(pieces):
    rows_in, weight_in, weight_out = pieces
    pre_act = low_back(highest(rows_in, weight_in))
    hidden = low(jax.nn.gelu(pre_act, approximate=True))
    return rounded_both(highest(hidden, weight_out))

def reference(tokens, w_query, w_key, w_value, w_attn_out, w_router, norm1_gain, norm2_gain, bias_table, w_expert_in, w_expert_out, routes, segments, cotangent):
    blocks = TOKENS // TOK_DEV
    route_ids = routes[:, 0].astype(jnp.int32)
    hot_blocks = route_ids.reshape(blocks, TOK_DEV)[:, :, None] == jnp.arange(EXPERTS, dtype=jnp.int32)[None, None, :]
    ranks = jnp.cumsum(hot_blocks.astype(jnp.int32), axis=1) - 1
    slot = lax.optimization_barrier(jnp.sum(jnp.where(hot_blocks, ranks, 0), axis=2)).reshape(TOKENS).astype(jnp.int32)
    owner = jnp.arange(TOKENS, dtype=jnp.int32) // TOK_DEV
    target = (route_ids * (blocks * CAP) + owner * CAP + slot).astype(jnp.int32)
    route_hot = (route_ids[:, None] == jnp.arange(EXPERTS, dtype=jnp.int32)[None, :]).astype(jnp.float32)
    doc_blocks = segments.reshape(blocks, TOK_DEV)

    def forward(token_f, wq, wk, wv, wo, wr, gain1, gain2, table, wi, wout):

        def one_block(pieces):
            return attend_block(pieces[0], pieces[1], wq, wk, wv, wo, gain1, table)
        mixed1 = lax.map(jax.checkpoint(one_block), (token_f.reshape(blocks, TOK_DEV, D), doc_blocks))
        mixed1 = mixed1.reshape(TOKENS, D)
        normed2 = low(rms_normed(mixed1, gain2))
        logits = low_back(highest(normed2, wr))
        router_probs = jax.nn.softmax(logits, axis=-1)
        gate = lax.optimization_barrier(jnp.sum(router_probs * route_hot, axis=1))
        placed = jnp.zeros((EXPERTS * blocks * CAP, D), jnp.float32).at[target].set(low_back(normed2))
        produced = lax.map(jax.checkpoint(expert_block), (placed.reshape(EXPERTS, blocks * CAP, D), wi, wout))
        expert_out = produced.reshape(EXPERTS * blocks * CAP, D)[target]
        return mixed1 + gate[:, None] * expert_out
    primals = tuple((item.astype(jnp.float32) for item in (tokens, w_query, w_key, w_value, w_attn_out, w_router, norm1_gain, norm2_gain, bias_table, w_expert_in, w_expert_out)))
    result, pullback = jax.vjp(forward, *primals)
    grads = pullback(cotangent.astype(jnp.float32))
    return (result.astype(jnp.bfloat16), grads[0], grads[1], grads[2], grads[3], grads[4], grads[5], grads[6], grads[7], grads[8], grads[9], grads[10])
```

```python
from functools import partial

import jax
import jax.numpy as jnp
import numpy as np
from jax import lax
from jax.experimental import pallas as pl
from jax.experimental.pallas import tpu as pltpu
from jax.sharding import PartitionSpec as P

eps = 1e-06
bucket_edges = (12, 16, 23, 32, 46, 64, 91)
f32 = jnp.float32
bf16 = jnp.bfloat16
i32 = jnp.int32
gelu_a = float(np.sqrt(2.0 / np.pi))
gelu_b = 0.044715

owner_of = (1, 2, 0, 3)


def nn(left, right):
    return lax.dot_general(left, right, (((1,), (0,)), ((), ())), preferred_element_type=f32)


def nt(left, right):
    return lax.dot_general(left, right, (((1,), (1,)), ((), ())), preferred_element_type=f32)


def tn(left, right):
    return lax.dot_general(left, right, (((0,), (0,)), ((), ())), preferred_element_type=f32)


def iota(shape, dim):
    return lax.broadcasted_iota(i32, shape, dim)


def call(body, outs, idx, *args, scratch=()):
    return pl.pallas_call(
        body,
        out_shape=[jax.ShapeDtypeStruct(s, d) for s, d in outs],
        in_specs=[pl.BlockSpec(memory_space=pltpu.SMEM)]
        + [pl.BlockSpec(memory_space=pltpu.VMEM)] * len(args),
        out_specs=[pl.BlockSpec(memory_space=pltpu.VMEM)] * len(outs),
        scratch_shapes=list(scratch),
        compiler_params=pltpu.CompilerParams(vmem_limit_bytes=40 * 1024 * 1024),
    )(idx, *args)


def rms_scale(values):
    return lax.rsqrt(jnp.mean(values * values, axis=-1, keepdims=True) + eps)


def norm_back(d_normed, normed, scale):
    return scale * (d_normed - normed * jnp.mean(d_normed * normed, axis=-1, keepdims=True))


def bucket_onehot(rows, length, centred):
    col = iota((rows, 2 * length), 1)
    n = (length - 1) - col if centred else jnp.where(col < length, -col, 2 * length - col)
    mag = jnp.abs(n)
    far = jnp.full_like(mag, 8)
    for threshold in bucket_edges:
        far = far + (mag >= threshold).astype(i32)
    bucket = jnp.where(n < 0, 16, 0) + jnp.where(mag < 8, mag, far)
    return (bucket == iota((rows, 2 * length), 0)).astype(f32).astype(bf16)


def pack_body(experts, smalls, idx, wq, wk, wv, wo, wr, g1, g2, tab, out):
    rows, width = wq.shape
    core = idx[2]

    @pl.when(core == 0)
    def _():
        out[0:rows, :] = wq[...]
        out[rows : 2 * rows, :] = wv[...]

    @pl.when(core == 1)
    def _():
        out[0:rows, :] = wk[...]
        out[rows : 2 * rows, :] = wo[...]

    heads = tab.shape[1]
    pick = (iota((smalls, experts), 0) == iota((smalls, experts), 1)).astype(f32).astype(bf16)
    part = nt(pick, wr[...])
    line = iota((smalls, rows), 0)
    part = part + jnp.where(line == experts, g1[...].astype(f32), 0.0)
    part = part + jnp.where(line == experts + 1, g2[...].astype(f32), 0.0)
    spread = (iota((rows, width), 0) == iota((rows, width), 1)).astype(f32).astype(bf16)
    whole = nn(part.astype(bf16), spread)
    pick_t = (iota((smalls, heads), 0) == iota((smalls, heads), 1) + experts + 2).astype(f32)
    table_t = nt(pick_t.astype(bf16), tab[...])
    shard = tab.shape[0]
    spread_t = (iota((shard, width), 0) + rows == iota((shard, width), 1)).astype(f32)
    whole = whole + nn(table_t.astype(bf16), spread_t.astype(bf16))
    out[2 * rows : 2 * rows + smalls, :] = whole.astype(bf16)


def place_body(experts, idx, consts, routes2, cot, cot_t, place, rows_out):
    me = idx[1]
    slots = place.shape[0]
    both = routes2.shape[1]
    half = both // 2
    route = routes2[...]
    hot = (iota((experts, both), 0) == route).astype(f32)
    a, b = iota((both, both), 0), iota((both, both), 1)
    earlier = ((a < b) & ((a < half) == (b < half))).astype(f32).astype(bf16)
    ranks = nn(hot.astype(bf16), earlier)
    slot = jnp.sum(hot * ranks, axis=0, keepdims=True).astype(i32)
    which = consts[:, 0:1] ^ me
    turn = consts[:, 1:2]
    number = consts[:, 2:3]
    side = (iota((slots, both), 1) >= half).astype(i32)
    hit = (which == route) & (number == slot) & (turn == side)
    placer = hit.astype(f32).astype(bf16)
    place[...] = placer
    rows = nn(placer[:, 0:half], cot[...]) + nn(placer[:, half:both], cot_t[...])
    rows_out[...] = rows.astype(bf16)


def place_rows_body(idx, place, own, other, rows_out):
    half = own.shape[0]
    rows = nn(place[:, 0:half], own[...]) + nn(place[:, half : 2 * half], other[...])
    rows_out[...] = rows.astype(bf16)


def unplace_body(idx, place, rows, own, other):
    half = own.shape[0]
    arrived = rows[...]
    own[...] = tn(place[:, 0:half], arrived)
    other[...] = tn(place[:, half : 2 * half], arrived).astype(bf16)


def attend_body(
    experts, smalls, heads, idx,
    tokens, seg_c, seg_r, routes_c, wq, wk, wv, wo, own, hx, hy, da, db, tx, ty, ta, tb,
    w_all, small_all, q_o, k_o, v_o, probs_o, ctx_o, mixed_o, hcat_o, rp_o,
):
    mine, core = idx[0], idx[2]
    rows, width = wq.shape
    length = tokens.shape[0]
    size = width // heads
    home = pl.multiple_of(mine * rows, 64)
    for m, w in enumerate((wq, wk, wv, wo)):
        w_all[m, pl.ds(home, rows), :] = w[...]
    for k, piece, held in ((1, hx, core), (2, hy, core), (1, tx, 1 - core), (2, ty, 1 - core)):
        at = pl.multiple_of((mine ^ k) * rows, 64)
        w_all[held, pl.ds(at, rows), :] = piece[0:rows, :]
        w_all[2 + held, pl.ds(at, rows), :] = piece[rows : 2 * rows, :]
    cut = da.shape[0]
    at = pl.multiple_of((mine ^ 3) * rows, 64)
    for first, second, held in ((da, db, core), (ta, tb, 1 - core)):
        w_all[held, pl.ds(at, rows), :] = first[0:rows, :]
        w_all[2 + held, pl.ds(at, cut - rows), :] = first[rows:cut, :]
        w_all[2 + held, pl.ds(at + (cut - rows), 2 * rows - cut), :] = second[0 : 2 * rows - cut, :]
    small = jnp.zeros((smalls, width), f32)
    table_t = jnp.zeros((smalls, 128), f32)
    shard = 32 // 4
    for k, piece, start in ((0, own, 2 * rows), (1, hx, 2 * rows), (2, hy, 2 * rows), (3, db, 2 * rows - cut)):
        j = mine ^ k
        part = piece[start : start + smalls, 0:256]
        r, c = iota((256, width), 0), iota((256, width), 1)
        small = small + nn(part, ((r < rows) & (c == r + rows * j)).astype(f32).astype(bf16))
        r, c = iota((256, 128), 0), iota((256, 128), 1)
        keep = (r >= rows) & (r < rows + shard) & (c == r - rows + shard * j)
        table_t = table_t + nn(part, keep.astype(f32).astype(bf16))
    small_all[...] = small
    gain1 = small[experts : experts + 1, :]
    gain2 = small[experts + 1 : experts + 2, :]
    per_offset = nn(table_t.astype(bf16), bucket_onehot(128, length, False))

    x = tokens[...].astype(f32)
    h1 = (x * rms_scale(x) * gain1).astype(bf16)
    q_o[...] = nn(h1, w_all[0]).astype(bf16)
    k_o[...] = nn(h1, w_all[1]).astype(bf16)
    v_o[...] = nn(h1, w_all[2]).astype(bf16)
    same = seg_c[...] == seg_r[...]
    low = iota((length, 2 * size), 1) < size
    zero = jnp.zeros((length, 2 * size), bf16)
    for p in range(heads // 2):
        cols = slice(2 * size * p, 2 * size * (p + 1))
        q2, k2, v2 = q_o[:, cols], k_o[:, cols], v_o[:, cols]
        got = []
        for t in range(2):
            h = 2 * p + t
            qh = jnp.where(low, q2, zero) if t == 0 else jnp.where(low, zero, q2)
            line = per_offset[experts + 2 + h : experts + 3 + h, :]
            bias = pltpu.roll(
                jnp.broadcast_to(line, (length, 2 * length)), 0, 1, stride=1, stride_axis=0
            )[:, 0:length]
            s = jnp.where(same, nt(qh, k2) + bias, -1000000000.0)
            e = jnp.exp(s - jnp.max(s, axis=-1, keepdims=True))
            pr = e / jnp.sum(e, axis=-1, keepdims=True)
            probs_o[h] = pr
            got.append(nn(pr.astype(bf16), v2))
        ctx_o[:, cols] = jnp.where(low, got[0], got[1]).astype(bf16)
    mixed = x + nn(ctx_o[...], w_all[3])
    mixed_o[...] = mixed
    h2 = (mixed * rms_scale(mixed) * gain2).astype(bf16)
    logits = nt(h2, small[0:experts, :].astype(bf16))
    e = jnp.exp(logits - jnp.max(logits, axis=-1, keepdims=True))
    rp = e / jnp.sum(e, axis=-1, keepdims=True)
    rp_o[...] = rp
    gate = jnp.sum(jnp.where(routes_c[...] == iota((length, experts), 1), rp, 0.0), axis=-1, keepdims=True)
    hcat_o[:, 0:width] = h2
    high = gate.astype(bf16).astype(f32)
    lane = iota((length, 128), 1)
    tail = jnp.where(lane == 0, high, jnp.where(lane == 1, gate - high, 0.0))
    hcat_o[:, width : width + 128] = tail.astype(bf16)


def back_in_body(idx, w_out, *refs):
    for k in range(4):
        refs[4][k] = nt(refs[k][...], w_out[...])


def expert_body(idx, w_in, g_all, x0, x1, x2, x3, y0, y1, y2, y3, hid_o, dpre_o):
    width = w_in.shape[0]
    lane = iota((x0.shape[0], 128), 1)
    for k, (x, y) in enumerate(((x0, y0), (x1, y1), (x2, y2), (x3, y3))):
        pre = nn(x[:, 0:width], w_in[...])
        tail = x[:, width : width + 128].astype(f32)
        gate = jnp.sum(jnp.where(lane < 2, tail, 0.0), axis=-1, keepdims=True)
        sq = pre * pre
        t = jnp.tanh(gelu_a * (pre + gelu_b * sq * pre))
        hid = (0.5 * pre * (1.0 + t)).astype(bf16)
        slope = 0.5 * (1.0 + t) + 0.5 * pre * (1.0 - t * t) * (gelu_a * (1.0 + 3.0 * gelu_b * sq))
        g = g_all[k]
        dpre = (gate * g * slope).astype(bf16)
        hid_o[k] = hid
        dpre_o[k] = dpre
        d_gate = jnp.sum(hid.astype(f32) * g, axis=-1, keepdims=True)
        y[:, 0:width] = nt(dpre, w_in[...]).astype(bf16)
        y[:, width : width + 128] = jnp.where(lane == 0, d_gate, 0.0).astype(bf16)


def expert_out_body(idx, w_out, hid, y0, y1, y2, y3):
    for k, y in enumerate((y0, y1, y2, y3)):
        y[...] = nn(hid[k], w_out[...]).astype(bf16)


def expert_grad_body(idx, hid, dpre, x0, x1, x2, x3, g0, g1, g2, g3, gi, go):
    width = gi.shape[1]
    lane = iota((x0.shape[0], 128), 1)
    acc_i = jnp.zeros((width, dpre.shape[2]), f32)
    for k, x in enumerate((x0, x1, x2, x3)):
        acc_i = acc_i + tn(x[:, 0:width], dpre[k])
    gi[0] = acc_i
    acc_o = jnp.zeros((hid.shape[2], width), f32)
    for k, (x, g) in enumerate(((x0, g0), (x1, g1), (x2, g2), (x3, g3))):
        tail = x[:, width : width + 128].astype(f32)
        gate = jnp.sum(jnp.where(lane < 2, tail, 0.0), axis=-1, keepdims=True)
        acc_o = acc_o + tn(hid[k], (gate * g[...].astype(f32)).astype(bf16))
    go[0] = acc_o


def attend_back_body(
    experts, heads, chips, idx,
    own, other, mixed_r, cot, rp_r, routes_c, small_all, w_all, q, k, v, probs, ctx,
    dmixed_o, d_o, router_o, gain2_o, table_o, *rest,
):
    turned, diag = rest[:-1], rest[-1]
    length, width = mixed_r.shape
    size = width // heads
    back = own[...] + other[...].astype(f32)
    lane = iota((length, 128), 1)
    d_gate = jnp.sum(jnp.where(lane == 0, back[:, width : width + 128], 0.0), axis=-1, keepdims=True)
    hot = (routes_c[...] == iota((length, experts), 1)).astype(f32)
    rp = rp_r[...]
    gate = jnp.sum(rp * hot, axis=-1, keepdims=True)
    d_logits = (rp * (hot - gate) * d_gate).astype(bf16)
    gain2 = small_all[experts + 1 : experts + 2, :]
    wr_t = small_all[0:experts, :].astype(bf16)
    mixed = mixed_r[...]
    scale2 = rms_scale(mixed)
    normed2 = mixed * scale2
    h2 = (normed2 * gain2).astype(bf16)
    router_o[...] = tn(d_logits, h2)
    d_h2 = nn(d_logits, wr_t) + back[:, 0:width]
    gain2_o[...] = jnp.sum(d_h2 * normed2, axis=0, keepdims=True)
    d_mixed = cot[...].astype(f32) + norm_back(d_h2 * gain2, normed2, scale2)
    dmixed_o[...] = d_mixed
    d_attn = d_mixed.astype(bf16)
    d_o[3] = d_attn
    d_ctx = nt(d_attn, w_all[3]).astype(bf16)
    low = iota((length, 2 * size), 1) < size
    zero = jnp.zeros((length, 2 * size), bf16)
    blank = jnp.zeros((length, length), f32)
    upside = iota((length, length), 0) + iota((length, length), 1) == length - 1
    upside = upside.astype(f32).astype(bf16)
    for p in range(heads // 2):
        cols = slice(2 * size * p, 2 * size * (p + 1))
        q2, k2, v2, c2 = q[:, cols], k[:, cols], v[:, cols], d_ctx[:, cols]
        gq, gk, gv = [], [], []
        for t in range(2):
            h = 2 * p + t
            ch = jnp.where(low, c2, zero) if t == 0 else jnp.where(low, zero, c2)
            pr = probs[h]
            dw = nt(ch, v2)
            gv.append(tn(pr.astype(bf16), c2))
            ds = (pr * (dw - jnp.sum(pr * dw, axis=-1, keepdims=True))).astype(bf16)
            gq.append(nn(ds, k2))
            gk.append(tn(ds, q2))
            wide = jnp.concatenate([nn(upside, ds), blank], axis=1)
            wide = pltpu.roll(wide, 0, 1, stride=1, stride_axis=0)
            diag[h : h + 1, :] = jnp.sum(wide, axis=0, keepdims=True)
        d_o[0, :, cols] = jnp.where(low, gq[0], gq[1]).astype(bf16)
        d_o[1, :, cols] = jnp.where(low, gk[0], gk[1]).astype(bf16)
        d_o[2, :, cols] = jnp.where(low, gv[0], gv[1]).astype(bf16)
    sums = diag[0:heads, :]
    onehot = bucket_onehot(128, length, True)
    high = sums.astype(bf16)
    mid = (sums - high.astype(f32)).astype(bf16)
    table_o[...] = nt(high, onehot) + nt(mid, onehot)
    if chips == 4:
        z = idx[3]
        for zr in range(4):
            dest = z ^ zr
            for m in range(4):

                @pl.when(dest == owner_of[m])
                def _():
                    turned[zr][...] = d_o[m]


def token_grad_body(experts, smalls, idx, tokens, dmixed, d, w_all, small_all, router, gain2, table, dtok_o, small_o, table_o):
    x = tokens[...].astype(f32)
    scale1 = rms_scale(x)
    normed1 = x * scale1
    gain1 = small_all[experts : experts + 1, :]
    d_h1 = nt(d[0], w_all[0]) + nt(d[1], w_all[1]) + nt(d[2], w_all[2])
    g_gain1 = jnp.sum(d_h1 * normed1, axis=0, keepdims=True)
    dtok_o[...] = dmixed[...] + norm_back(d_h1 * gain1, normed1, scale1)
    width = x.shape[1]
    pick = (iota((smalls, experts), 0) == iota((smalls, experts), 1)).astype(f32).astype(bf16)
    line = iota((smalls, width), 0)
    out = nn(pick, router[...].astype(bf16))
    out = out + jnp.where(line == experts, g_gain1, 0.0) + jnp.where(line == experts + 1, gain2[...], 0.0)
    small_o[...] = out.astype(bf16)
    heads = table.shape[0]
    pick_t = (iota((smalls, heads), 0) == iota((smalls, heads), 1) + experts + 2).astype(f32)
    table_o[...] = nn(pick_t.astype(bf16), table[...].astype(bf16)).astype(bf16)


def mixer_grad_body(experts, idx, small_all, l0, l1, l2, l3, c0, c1, c2, c3, d0, d1, d2, d3, keep, send, acc, left):
    z, core = idx[3], idx[2]
    gain1 = small_all[experts : experts + 1, :]
    rows = l0.shape[0]

    @pl.when(z == owner_of[3])
    def _():
        for n, c in enumerate((c0, c1, c2, c3)):
            left[n * rows : (n + 1) * rows, :] = c[...]

    @pl.when(z != owner_of[3])
    def _():
        for n, item in enumerate((l0, l1, l2, l3)):
            x = item[...].astype(f32)
            left[n * rows : (n + 1) * rows, :] = (x * rms_scale(x) * gain1).astype(bf16)

    right = jnp.concatenate([d0[...], d1[...], d2[...], d3[...]], axis=0)
    acc[...] = tn(left[...], right)
    half = keep.shape[1]
    keep[...] = acc[:, pl.ds(pl.multiple_of(core * half, 128), half)]
    send[...] = acc[:, pl.ds(pl.multiple_of((1 - core) * half, 128), half)].astype(bf16)


def share_body(shard, idx, keep, got, small, table, s0, s1, s2, s3, total):
    mine = idx[0]
    total[...] = keep[...] + got[...].astype(f32)
    half = keep.shape[1]
    rows = total.shape[0] // 4
    width = small.shape[1]
    for k, out in enumerate((s0, s1, s2, s3)):
        j = mine ^ k
        out[0:rows, :] = total[pl.ds(pl.multiple_of(j * rows, 64), rows), :].astype(bf16)
        r, c = iota((width, half), 0), iota((width, half), 1)
        part = nn(small[...], ((c < rows) & (r == c + rows * j)).astype(f32).astype(bf16))
        r, c = iota((128, half), 0), iota((128, half), 1)
        keep_t = (c >= rows) & (c < rows + shard) & (r == c - rows + shard * j)
        part = part + nn(table[...], keep_t.astype(f32).astype(bf16))
        out[rows : rows + small.shape[0], :] = part.astype(bf16)


def sum_body(idx, a, b, c, d, out):
    out[...] = (
        a[...].astype(f32) + b[...].astype(f32) + c[...].astype(f32) + d[...].astype(f32)
    ).astype(bf16)


def finish_body(idx, a0, a1, a2, a3, b0, b1, b2, b3, gq, gk, gv, go, small):
    z, core = idx[3], idx[2]
    half = a0.shape[1]
    rows = gq.shape[0]
    at = pl.multiple_of(core * half, 128)
    off = pl.multiple_of((1 - core) * half, 128)
    for m, out in enumerate((gq, gk, gv, go)):
        for zr, (a, b) in enumerate(((a0, b0), (a1, b1), (a2, b2), (a3, b3))):

            @pl.when((z ^ zr) == owner_of[m])
            def _():
                out[:, pl.ds(at, half)] = a[0:rows, :].astype(f32)
                out[:, pl.ds(off, half)] = b[0:rows, :].astype(f32)

    total = jnp.zeros(small.shape, f32)
    for item in (a0, a1, a2, a3, b0, b1, b2, b3):
        total = total + item[rows : rows + small.shape[0], :].astype(f32)
    small[...] = total


def on_device(
    tokens, w_query, w_key, w_value, w_attn_out, w_router, norm1_gain, norm2_gain, bias_table,
    w_expert_in, w_expert_out, routes, segments, cotangent,
):
    experts = lax.axis_size("expert")
    chips = experts // 2
    length, width = tokens.shape
    heads = bias_table.shape[1]
    rows = w_query.shape[0]
    shard = bias_table.shape[0]
    cap = 5 * length // (4 * experts)
    smalls = -(-(experts + 2 + heads) // 16) * 16
    slots = experts * cap
    wide = width + 128

    def along(x, axis, mask):
        n = lax.axis_size(axis)
        return lax.ppermute(x, axis, [(s, s ^ mask) for s in range(n)])

    def twin(x):
        return along(x, "expert", 1)

    def chip_exchange(x):
        cut = 2 * cap
        parts = [x[0:cut]]
        for zr in range(1, chips):
            parts.append(along(x[cut * zr : cut * (zr + 1)], "expert", 2 * zr))
        return jnp.concatenate(parts, axis=0)

    mine, me = lax.axis_index("dp"), lax.axis_index("expert")
    idx = jnp.stack([mine, me, me % 2, me // 2]).astype(i32)
    weight_in, weight_out = w_expert_in[0], w_expert_out[0]

    parcel = call(
        partial(pack_body, experts, smalls), [((2 * rows + smalls, width), bf16)], idx,
        w_query, w_key, w_value, w_attn_out, w_router, norm1_gain[None], norm2_gain[None], bias_table,
    )[0]
    cut = (2 * rows + smalls) // 2
    hx = along(parcel, "dp", 1)
    hy = along(parcel, "dp", 2)
    da = along(hx[0:cut], "dp", 2)
    db = along(hy[cut:], "dp", 1)
    tx, ty, ta, tb = twin(hx), twin(hy), twin(da), twin(db)

    route_row = routes.reshape(1, length)
    routes2 = jnp.concatenate([route_row, twin(route_row.astype(f32)).astype(i32)], axis=1)
    r = np.arange(slots)
    consts = np.zeros((slots, 128), np.int32)
    consts[:, 0] = 2 * (r // (2 * cap))
    consts[:, 1] = (r // cap) % 2
    consts[:, 2] = r % cap
    place, g_rows = call(
        partial(place_body, experts), [((slots, 2 * length), bf16), ((slots, width), bf16)], idx,
        jnp.asarray(consts), routes2, cotangent, twin(cotangent),
    )
    g_here = chip_exchange(g_rows)
    g_set = [g_here] + [along(g_here, "dp", k) for k in (1, 2, 3)]
    g_back = call(back_in_body, [((4, slots, width), f32)], idx, weight_out, *g_set)[0]

    if chips == 4:
        tok_all = [tokens] + [along(tokens, "expert", 2 * zr) for zr in range(1, 4)]

    w_all, small_all, q, k, v, probs, ctx, mixed, hcat, rp = call(
        partial(attend_body, experts, smalls, heads),
        [
            ((4, width, width), bf16), ((smalls, width), f32),
            ((length, width), bf16), ((length, width), bf16), ((length, width), bf16),
            ((heads, length, length), f32), ((length, width), bf16), ((length, width), f32),
            ((length, wide), bf16), ((length, experts), f32),
        ],
        idx, tokens, segments.reshape(length, 1), segments.reshape(1, length), routes,
        w_query, w_key, w_value, w_attn_out, parcel, hx, hy, da, db, tx, ty, ta, tb,
    )

    x_rows = call(place_rows_body, [((slots, wide), bf16)], idx, place, hcat, twin(hcat))[0]
    x_here = chip_exchange(x_rows)
    x_set = [x_here] + [along(x_here, "dp", kk) for kk in (1, 2, 3)]
    *d_parts, hid, dpre = call(
        expert_body,
        [((slots, wide), bf16)] * 4 + [((4, slots, width), bf16)] * 2,
        idx, weight_in, g_back, *x_set,
    )
    d_got = [d_parts[0]] + [along(d_parts[kk], "dp", kk) for kk in (1, 2, 3)]
    d_here = call(sum_body, [((slots, wide), bf16)], idx, *d_got)[0]
    d_rows = chip_exchange(d_here)
    back_own, back_other = call(
        unplace_body, [((length, wide), f32), ((length, wide), bf16)], idx, place, d_rows
    )
    back_other = twin(back_other)

    outs = [
        ((length, width), f32), ((4, length, width), bf16), ((experts, width), f32),
        ((1, width), f32), ((heads, 128), f32),
    ]
    if chips == 4:
        outs = outs + [((length, width), bf16)] * 4
    d_mixed, d_all, g_router, g_gain2, g_table, *turned = call(
        partial(attend_back_body, experts, heads, chips), outs, idx,
        back_own, back_other, mixed, cotangent, rp, routes, small_all, w_all, q, k, v, probs, ctx,
        scratch=[pltpu.VMEM((16, 2 * length), f32)],
    )
    d_tokens, small_g, table_g = call(
        partial(token_grad_body, experts, smalls),
        [((length, width), f32), ((smalls, width), bf16), ((smalls, 128), bf16)], idx,
        tokens, d_mixed, d_all, w_all, small_all, g_router, g_gain2, g_table,
    )

    y_parts = call(expert_out_body, [((slots, width), bf16)] * 4, idx, weight_out, hid)
    y_got = [y_parts[0]] + [along(y_parts[kk], "dp", kk) for kk in (1, 2, 3)]
    y_here = call(sum_body, [((slots, width), bf16)], idx, *y_got)[0]
    y_rows = chip_exchange(y_here)
    y_own, y_other = call(
        unplace_body, [((length, width), f32), ((length, width), bf16)], idx, place, y_rows
    )
    y_other = twin(y_other)
    gate = jnp.sum(jnp.where(routes == jnp.arange(experts, dtype=i32)[None, :], rp, 0.0), axis=1, keepdims=True)
    layer_out = (mixed + gate * (y_own + y_other.astype(f32))).astype(bf16)

    grad_in, grad_out = call(
        expert_grad_body,
        [((1, width, weight_in.shape[1]), f32), ((1, weight_out.shape[0], width), f32)], idx,
        hid, dpre, *x_set, *g_set,
    )

    if chips == 4:
        ctx_all = [ctx] + [along(ctx, "expert", 2 * zr) for zr in range(1, 4)]
        d_in = [turned[0]] + [along(turned[zr], "expert", 2 * zr) for zr in range(1, 4)]
        keep, send = call(
            partial(mixer_grad_body, experts),
            [((width, width // 2), f32), ((width, width // 2), bf16)], idx,
            small_all, *tok_all, *ctx_all, *d_in,
            scratch=[pltpu.VMEM((width, width), f32), pltpu.VMEM((4 * length, width), bf16)],
        )
        parts = call(
            partial(share_body, shard), [((rows + smalls, width // 2), bf16)] * 4, idx,
            keep, twin(send), small_g, table_g, scratch=[pltpu.VMEM((width, width // 2), f32)],
        )
        got = [parts[0]] + [along(parts[kk], "dp", kk) for kk in (1, 2, 3)]
        total = call(sum_body, [((rows + smalls, width // 2), bf16)], idx, *got)[0]
        a_set = [total] + [along(total, "expert", 2 * zr) for zr in range(1, 4)]
        b_set = [twin(a) for a in a_set]
        g_q, g_k, g_v, g_o, small_t = call(
            finish_body, [((rows, width), f32)] * 4 + [((smalls, width // 2), f32)], idx, *a_set, *b_set
        )
        r_out = small_t[0:experts, 0:rows].T
        gain1_out = small_t[experts, 0:rows]
        gain2_out = small_t[experts + 1, 0:rows]
        table_out = small_t[experts + 2 : experts + 2 + heads, rows : rows + shard].T
    else:
        gain1 = small_all[experts : experts + 1]
        x = tokens.astype(f32)
        h1 = (x * rms_scale(x) * gain1).astype(bf16)
        both = jnp.concatenate(
            [tn(h1, d_all[0]), tn(h1, d_all[1]), tn(h1, d_all[2]), tn(ctx, d_all[3]), small_g.T.astype(f32)], axis=1
        )
        both = lax.psum_scatter(both, "dp", scatter_dimension=0, tiled=True)
        both = lax.psum(both, "expert")
        g_q, g_k, g_v, g_o = (both[:, m * width : (m + 1) * width] for m in range(4))
        rest = both[:, 4 * width :]
        r_out = rest[:, 0:experts]
        gain1_out, gain2_out = rest[:, experts], rest[:, experts + 1]
        tab = table_g.T[0 : 4 * shard, experts + 2 : experts + 2 + heads].astype(f32)
        table_out = lax.psum(lax.psum_scatter(tab, "dp", scatter_dimension=0, tiled=True), "expert")
    return (
        layer_out, d_tokens, g_q, g_k, g_v, g_o, r_out, gain1_out, gain2_out, table_out, grad_in, grad_out,
    )


def solution(mesh):
    return jax.shard_map(
        on_device,
        mesh=mesh,
        in_specs=(
            P(("dp", "expert"), None),
            P("dp", None),
            P("dp", None),
            P("dp", None),
            P("dp", None),
            P("dp", None),
            P("dp"),
            P("dp"),
            P("dp", None),
            P("expert", None, "dp"),
            P("expert", "dp", None),
            P(("dp", "expert"), None),
            P(("dp", "expert")),
            P(("dp", "expert"), None),
        ),
        out_specs=(
            P(("dp", "expert"), None),
            P(("dp", "expert"), None),
            P("dp", None),
            P("dp", None),
            P("dp", None),
            P("dp", None),
            P("dp", None),
            P("dp"),
            P("dp"),
            P("dp", None),
            P("expert", None, "dp"),
            P("expert", "dp", None),
        ),
        check_vma=False,
    )
```

```python
from functools import partial

import jax
import jax.numpy as jnp
import numpy as np
from jax import lax
from jax.experimental import pallas as pl
from jax.experimental.pallas import tpu as pltpu
from jax.sharding import PartitionSpec as P

eps = 1e-06
bucket_edges = (12, 16, 23, 32, 46, 64, 91)
f32 = jnp.float32
bf16 = jnp.bfloat16
i32 = jnp.int32
gelu_a = float(np.sqrt(2.0 / np.pi))
gelu_b = 0.044715

owner_of = (1, 2, 0, 3)


def nn(left, right):
    return lax.dot_general(left, right, (((1,), (0,)), ((), ())), preferred_element_type=f32)


def nt(left, right):
    return lax.dot_general(left, right, (((1,), (1,)), ((), ())), preferred_element_type=f32)


def tn(left, right):
    return lax.dot_general(left, right, (((0,), (0,)), ((), ())), preferred_element_type=f32)


def iota(shape, dim):
    return lax.broadcasted_iota(i32, shape, dim)


def after(value, *earlier):
    return lax.optimization_barrier((value, *earlier))[0]


def call(name, micros, body, outs, idx, *args, scratch=()):
    return pl.pallas_call(
        body,
        name=name,
        cost_estimate=pl.CostEstimate(flops=int(micros * 1.1e9), bytes_accessed=int(micros * 1e6), transcendentals=0),
        out_shape=[jax.ShapeDtypeStruct(s, d) for s, d in outs],
        in_specs=[pl.BlockSpec(memory_space=pltpu.SMEM)]
        + [pl.BlockSpec(memory_space=pltpu.VMEM)] * len(args),
        out_specs=[pl.BlockSpec(memory_space=pltpu.VMEM)] * len(outs),
        scratch_shapes=list(scratch),
        compiler_params=pltpu.CompilerParams(vmem_limit_bytes=40 * 1024 * 1024),
    )(idx, *args)


def rms_scale(values):
    return lax.rsqrt(jnp.mean(values * values, axis=-1, keepdims=True) + eps)


def norm_back(d_normed, normed, scale):
    return scale * (d_normed - normed * jnp.mean(d_normed * normed, axis=-1, keepdims=True))


def bucket_onehot(rows, length, centred):
    col = iota((rows, 2 * length), 1)
    n = (length - 1) - col if centred else jnp.where(col < length, -col, 2 * length - col)
    mag = jnp.abs(n)
    far = jnp.full_like(mag, 8)
    for threshold in bucket_edges:
        far = far + (mag >= threshold).astype(i32)
    bucket = jnp.where(n < 0, 16, 0) + jnp.where(mag < 8, mag, far)
    return (bucket == iota((rows, 2 * length), 0)).astype(f32).astype(bf16)


def pack_body(experts, smalls, idx, wr_t, g1, g2, tab, out):
    rows = wr_t.shape[1]
    heads, shard = tab.shape[1], tab.shape[0]
    pick = (iota((smalls, experts), 0) == iota((smalls, experts), 1)).astype(f32).astype(bf16)
    part = nn(pick, wr_t[...])
    line = iota((smalls, rows), 0)
    part = part + jnp.where(line == experts, g1[...].astype(f32), 0.0)
    part = part + jnp.where(line == experts + 1, g2[...].astype(f32), 0.0)
    width = out.shape[1]
    spread = (iota((rows, width), 0) == iota((rows, width), 1)).astype(f32).astype(bf16)
    whole = nn(part.astype(bf16), spread)
    pick_t = (iota((smalls, heads), 0) == iota((smalls, heads), 1) + experts + 2).astype(f32)
    table_t = nt(pick_t.astype(bf16), tab[...])
    spread_t = (iota((shard, width), 0) + rows == iota((shard, width), 1)).astype(f32)
    whole = whole + nn(table_t.astype(bf16), spread_t.astype(bf16))
    out[...] = whole.astype(bf16)


def place_body(experts, idx, consts, routes2, cot, cot_t, place, rows_out):
    me = idx[1]
    slots = place.shape[0]
    both = routes2.shape[1]
    half = both // 2
    route = routes2[...]
    hot = (iota((experts, both), 0) == route).astype(f32)
    a, b = iota((both, both), 0), iota((both, both), 1)
    earlier = ((a < b) & ((a < half) == (b < half))).astype(f32).astype(bf16)
    ranks = nn(hot.astype(bf16), earlier)
    slot = jnp.sum(hot * ranks, axis=0, keepdims=True).astype(i32)
    which = consts[:, 0:1] ^ me
    turn = consts[:, 1:2]
    number = consts[:, 2:3]
    side = (iota((slots, both), 1) >= half).astype(i32)
    hit = (which == route) & (number == slot) & (turn == side)
    placer = hit.astype(f32).astype(bf16)
    place[...] = placer
    rows = nn(placer[:, 0:half], cot[...]) + nn(placer[:, half:both], cot_t[...])
    rows_out[...] = rows.astype(bf16)


def place_rows_body(idx, place, own, other, rows_out):
    half = own.shape[0]
    rows = nn(place[:, 0:half], own[...]) + nn(place[:, half : 2 * half], other[...])
    rows_out[...] = rows.astype(bf16)


def unplace_body(idx, place, rows, own, other):
    half = own.shape[0]
    arrived = rows[...]
    own[...] = tn(place[:, 0:half], arrived)
    other[...] = tn(place[:, half : 2 * half], arrived).astype(bf16)


def attend_body(
    experts, smalls, heads, idx,
    tokens, seg_c, seg_r, routes_c, wq, wk, wv, wo, s0, s1, hx, hy, da, db, tx, ty, ta, tb,
    w_all, small_all, q_o, k_o, v_o, probs_o, ctx_o, mixed_o, hcat_o, rp_o, *left,
):
    mine, core = idx[0], idx[2]
    rows, width = wq.shape
    length = tokens.shape[0]
    size = width // heads
    home = pl.multiple_of(mine * rows, 64)
    for m, w in enumerate((wq, wk, wv, wo)):
        w_all[m, pl.ds(home, rows), :] = w[...]
    for k, piece, held in ((1, hx, core), (2, hy, core), (1, tx, 1 - core), (2, ty, 1 - core)):
        at = pl.multiple_of((mine ^ k) * rows, 64)
        w_all[held, pl.ds(at, rows), :] = piece[0:rows, :]
        w_all[2 + held, pl.ds(at, rows), :] = piece[rows : 2 * rows, :]
    at = pl.multiple_of((mine ^ 3) * rows, 64)
    for first, second, held in ((da, db, core), (ta, tb, 1 - core)):
        w_all[held, pl.ds(at, rows), :] = first[0:rows, :]
        w_all[2 + held, pl.ds(at, rows), :] = second[...]
    small = jnp.zeros((smalls, width), f32)
    table_t = jnp.zeros((smalls, 128), f32)
    shard = 32 // 4
    for k, piece, start in ((0, s0, 0), (1, s1, 0), (2, da, rows), (3, da, rows + smalls)):
        j = mine ^ k
        part = piece[start : start + smalls, 0:256]
        r, c = iota((256, width), 0), iota((256, width), 1)
        small = small + nn(part, ((r < rows) & (c == r + rows * j)).astype(f32).astype(bf16))
        r, c = iota((256, 128), 0), iota((256, 128), 1)
        keep = (r >= rows) & (r < rows + shard) & (c == r - rows + shard * j)
        table_t = table_t + nn(part, keep.astype(f32).astype(bf16))
    small_all[...] = small
    gain1 = small[experts : experts + 1, :]
    gain2 = small[experts + 1 : experts + 2, :]
    per_offset = nn(table_t.astype(bf16), bucket_onehot(128, length, False))

    x = tokens[...].astype(f32)
    h1 = (x * rms_scale(x) * gain1).astype(bf16)
    q_o[...] = nn(h1, w_all[0]).astype(bf16)
    k_o[...] = nn(h1, w_all[1]).astype(bf16)
    v_o[...] = nn(h1, w_all[2]).astype(bf16)
    same = seg_c[...] == seg_r[...]
    low = iota((length, 2 * size), 1) < size
    zero = jnp.zeros((length, 2 * size), bf16)
    for p in range(heads // 2):
        cols = slice(2 * size * p, 2 * size * (p + 1))
        q2, k2, v2 = q_o[:, cols], k_o[:, cols], v_o[:, cols]
        got = []
        for t in range(2):
            h = 2 * p + t
            qh = jnp.where(low, q2, zero) if t == 0 else jnp.where(low, zero, q2)
            line = per_offset[experts + 2 + h : experts + 3 + h, :]
            bias = pltpu.roll(
                jnp.broadcast_to(line, (length, 2 * length)), 0, 1, stride=1, stride_axis=0
            )[:, 0:length]
            s = jnp.where(same, nt(qh, k2) + bias, -1000000000.0)
            e = jnp.exp(s - jnp.max(s, axis=-1, keepdims=True))
            pr = e / jnp.sum(e, axis=-1, keepdims=True)
            probs_o[h] = pr
            got.append(nn(pr.astype(bf16), v2))
        ctx_o[:, cols] = jnp.where(low, got[0], got[1]).astype(bf16)
    mixed = x + nn(ctx_o[...], w_all[3])
    mixed_o[...] = mixed
    h2 = (mixed * rms_scale(mixed) * gain2).astype(bf16)
    logits = nt(h2, small[0:experts, :].astype(bf16))
    e = jnp.exp(logits - jnp.max(logits, axis=-1, keepdims=True))
    rp = e / jnp.sum(e, axis=-1, keepdims=True)
    rp_o[...] = rp
    gate = jnp.sum(jnp.where(routes_c[...] == iota((length, experts), 1), rp, 0.0), axis=-1, keepdims=True)
    hcat_o[:, 0:width] = h2
    high = gate.astype(bf16).astype(f32)
    lane = iota((length, 128), 1)
    tail = jnp.where(lane == 0, high, jnp.where(lane == 1, gate - high, 0.0))
    hcat_o[:, width : width + 128] = tail.astype(bf16)
    for zr, item in enumerate(left):

        @pl.when((idx[3] ^ zr) == owner_of[3])
        def _():
            item[...] = ctx_o[...]

        @pl.when((idx[3] ^ zr) != owner_of[3])
        def _():
            item[...] = tokens[...]


def back_in_body(idx, w_out, *refs):
    for k in range(4):
        refs[4][k] = nt(refs[k][...], w_out[...])


def expert_body(idx, w_in, g_all, x0, x1, x2, x3, y0, y1, y2, y3, hid_o, dpre_o):
    width = w_in.shape[0]
    lane = iota((x0.shape[0], 128), 1)
    for k, (x, y) in enumerate(((x0, y0), (x1, y1), (x2, y2), (x3, y3))):
        pre = nn(x[:, 0:width], w_in[...])
        tail = x[:, width : width + 128].astype(f32)
        gate = jnp.sum(jnp.where(lane < 2, tail, 0.0), axis=-1, keepdims=True)
        sq = pre * pre
        t = jnp.tanh(gelu_a * (pre + gelu_b * sq * pre))
        hid = (0.5 * pre * (1.0 + t)).astype(bf16)
        slope = 0.5 * (1.0 + t) + 0.5 * pre * (1.0 - t * t) * (gelu_a * (1.0 + 3.0 * gelu_b * sq))
        g = g_all[k]
        dpre = (gate * g * slope).astype(bf16)
        hid_o[k] = hid
        dpre_o[k] = dpre
        d_gate = jnp.sum(hid.astype(f32) * g, axis=-1, keepdims=True)
        y[:, 0:width] = nt(dpre, w_in[...]).astype(bf16)
        y[:, width : width + 128] = jnp.where(lane == 0, d_gate, 0.0).astype(bf16)


def expert_out_body(idx, w_out, hid, y0, y1, y2, y3):
    for k, y in enumerate((y0, y1, y2, y3)):
        y[...] = nn(hid[k], w_out[...]).astype(bf16)


def expert_grad_body(idx, hid, dpre, x0, x1, x2, x3, g0, g1, g2, g3, gi, go):
    width = gi.shape[1]
    lane = iota((x0.shape[0], 128), 1)
    acc_i = jnp.zeros((width, dpre.shape[2]), f32)
    for k, x in enumerate((x0, x1, x2, x3)):
        acc_i = acc_i + tn(x[:, 0:width], dpre[k])
    gi[0] = acc_i
    acc_o = jnp.zeros((hid.shape[2], width), f32)
    for k, (x, g) in enumerate(((x0, g0), (x1, g1), (x2, g2), (x3, g3))):
        tail = x[:, width : width + 128].astype(f32)
        gate = jnp.sum(jnp.where(lane < 2, tail, 0.0), axis=-1, keepdims=True)
        acc_o = acc_o + tn(hid[k], (gate * g[...].astype(f32)).astype(bf16))
    go[0] = acc_o


def attend_back_body(
    experts, heads, chips, idx,
    own, other, mixed_r, cot, rp_r, routes_c, small_all, w_all, q, k, v, probs, ctx,
    dmixed_o, d_o, router_o, gain2_o, table_o, *rest,
):
    turned, diag = rest[:-1], rest[-1]
    length, width = mixed_r.shape
    size = width // heads
    back = own[...] + other[...].astype(f32)
    lane = iota((length, 128), 1)
    d_gate = jnp.sum(jnp.where(lane == 0, back[:, width : width + 128], 0.0), axis=-1, keepdims=True)
    hot = (routes_c[...] == iota((length, experts), 1)).astype(f32)
    rp = rp_r[...]
    gate = jnp.sum(rp * hot, axis=-1, keepdims=True)
    d_logits = (rp * (hot - gate) * d_gate).astype(bf16)
    gain2 = small_all[experts + 1 : experts + 2, :]
    wr_t = small_all[0:experts, :].astype(bf16)
    mixed = mixed_r[...]
    scale2 = rms_scale(mixed)
    normed2 = mixed * scale2
    h2 = (normed2 * gain2).astype(bf16)
    router_o[...] = tn(d_logits, h2)
    d_h2 = nn(d_logits, wr_t) + back[:, 0:width]
    gain2_o[...] = jnp.sum(d_h2 * normed2, axis=0, keepdims=True)
    d_mixed = cot[...].astype(f32) + norm_back(d_h2 * gain2, normed2, scale2)
    dmixed_o[...] = d_mixed
    d_attn = d_mixed.astype(bf16)
    d_o[3] = d_attn
    d_ctx = nt(d_attn, w_all[3]).astype(bf16)
    low = iota((length, 2 * size), 1) < size
    zero = jnp.zeros((length, 2 * size), bf16)
    blank = jnp.zeros((length, length), f32)
    upside = iota((length, length), 0) + iota((length, length), 1) == length - 1
    upside = upside.astype(f32).astype(bf16)
    for p in range(heads // 2):
        cols = slice(2 * size * p, 2 * size * (p + 1))
        q2, k2, v2, c2 = q[:, cols], k[:, cols], v[:, cols], d_ctx[:, cols]
        gq, gk, gv = [], [], []
        for t in range(2):
            h = 2 * p + t
            ch = jnp.where(low, c2, zero) if t == 0 else jnp.where(low, zero, c2)
            pr = probs[h]
            dw = nt(ch, v2)
            gv.append(tn(pr.astype(bf16), c2))
            ds = (pr * (dw - jnp.sum(pr * dw, axis=-1, keepdims=True))).astype(bf16)
            gq.append(nn(ds, k2))
            gk.append(tn(ds, q2))
            wide = jnp.concatenate([nn(upside, ds), blank], axis=1)
            wide = pltpu.roll(wide, 0, 1, stride=1, stride_axis=0)
            diag[h : h + 1, :] = jnp.sum(wide, axis=0, keepdims=True)
        d_o[0, :, cols] = jnp.where(low, gq[0], gq[1]).astype(bf16)
        d_o[1, :, cols] = jnp.where(low, gk[0], gk[1]).astype(bf16)
        d_o[2, :, cols] = jnp.where(low, gv[0], gv[1]).astype(bf16)
    sums = diag[0:heads, :]
    onehot = bucket_onehot(128, length, True)
    high = sums.astype(bf16)
    mid = (sums - high.astype(f32)).astype(bf16)
    table_o[...] = nt(high, onehot) + nt(mid, onehot)
    if chips == 4:
        z = idx[3]
        for zr in range(4):
            dest = z ^ zr
            for m in range(4):

                @pl.when(dest == owner_of[m])
                def _():
                    turned[zr][...] = d_o[m]


def token_grad_body(experts, smalls, idx, tokens, dmixed, d, w_all, small_all, router, gain2, table, dtok_o, small_o, table_o):
    x = tokens[...].astype(f32)
    scale1 = rms_scale(x)
    normed1 = x * scale1
    gain1 = small_all[experts : experts + 1, :]
    d_h1 = nt(d[0], w_all[0]) + nt(d[1], w_all[1]) + nt(d[2], w_all[2])
    g_gain1 = jnp.sum(d_h1 * normed1, axis=0, keepdims=True)
    dtok_o[...] = dmixed[...] + norm_back(d_h1 * gain1, normed1, scale1)
    width = x.shape[1]
    pick = (iota((smalls, experts), 0) == iota((smalls, experts), 1)).astype(f32).astype(bf16)
    line = iota((smalls, width), 0)
    out = nn(pick, router[...].astype(bf16))
    out = out + jnp.where(line == experts, g_gain1, 0.0) + jnp.where(line == experts + 1, gain2[...], 0.0)
    small_o[...] = out.astype(bf16)
    heads = table.shape[0]
    pick_t = (iota((smalls, heads), 0) == iota((smalls, heads), 1) + experts + 2).astype(f32)
    table_o[...] = nn(pick_t.astype(bf16), table[...].astype(bf16)).astype(bf16)


def mixer_grad_body(experts, idx, small_all, l0, l1, l2, l3, d0, d1, d2, d3, keep, send, acc, left):
    z, core = idx[3], idx[2]
    gain1 = small_all[experts : experts + 1, :]
    rows = l0.shape[0]

    @pl.when(z == owner_of[3])
    def _():
        for n, c in enumerate((l0, l1, l2, l3)):
            left[n * rows : (n + 1) * rows, :] = c[...]

    @pl.when(z != owner_of[3])
    def _():
        for n, item in enumerate((l0, l1, l2, l3)):
            x = item[...].astype(f32)
            left[n * rows : (n + 1) * rows, :] = (x * rms_scale(x) * gain1).astype(bf16)

    right = jnp.concatenate([d0[...], d1[...], d2[...], d3[...]], axis=0)
    acc[...] = tn(left[...], right)
    half = keep.shape[1]
    keep[...] = acc[:, pl.ds(pl.multiple_of(core * half, 128), half)]
    send[...] = acc[:, pl.ds(pl.multiple_of((1 - core) * half, 128), half)].astype(bf16)


def share_body(shard, idx, keep, got, small, table, s0, s1, s2, s3, total):
    mine = idx[0]
    total[...] = keep[...] + got[...].astype(f32)
    half = keep.shape[1]
    rows = total.shape[0] // 4
    width = small.shape[1]
    for k, out in enumerate((s0, s1, s2, s3)):
        j = mine ^ k
        out[0:rows, :] = total[pl.ds(pl.multiple_of(j * rows, 64), rows), :].astype(bf16)
        r, c = iota((width, half), 0), iota((width, half), 1)
        part = nn(small[...], ((c < rows) & (r == c + rows * j)).astype(f32).astype(bf16))
        r, c = iota((128, half), 0), iota((128, half), 1)
        keep_t = (c >= rows) & (c < rows + shard) & (r == c - rows + shard * j)
        part = part + nn(table[...], keep_t.astype(f32).astype(bf16))
        out[rows : rows + small.shape[0], :] = part.astype(bf16)


def sum_body(idx, a, b, c, d, out):
    out[...] = (
        a[...].astype(f32) + b[...].astype(f32) + c[...].astype(f32) + d[...].astype(f32)
    ).astype(bf16)


def finish_body(idx, a0, a1, a2, a3, b0, b1, b2, b3, gq, gk, gv, go, small):
    z, core = idx[3], idx[2]
    half = a0.shape[1]
    rows = gq.shape[0]
    at = pl.multiple_of(core * half, 128)
    off = pl.multiple_of((1 - core) * half, 128)
    for m, out in enumerate((gq, gk, gv, go)):
        for zr, (a, b) in enumerate(((a0, b0), (a1, b1), (a2, b2), (a3, b3))):

            @pl.when((z ^ zr) == owner_of[m])
            def _():
                out[:, pl.ds(at, half)] = a[0:rows, :].astype(f32)
                out[:, pl.ds(off, half)] = b[0:rows, :].astype(f32)

    total = jnp.zeros(small.shape, f32)
    for item in (a0, a1, a2, a3, b0, b1, b2, b3):
        total = total + item[rows : rows + small.shape[0], :].astype(f32)
    small[...] = total


def on_device(
    tokens, w_query, w_key, w_value, w_attn_out, w_router, norm1_gain, norm2_gain, bias_table,
    w_expert_in, w_expert_out, routes, segments, cotangent,
):
    experts = lax.axis_size("expert")
    chips = experts // 2
    length, width = tokens.shape
    heads = bias_table.shape[1]
    rows = w_query.shape[0]
    shard = bias_table.shape[0]
    cap = 5 * length // (4 * experts)
    smalls = -(-(experts + 2 + heads) // 16) * 16
    slots = experts * cap
    wide = width + 128

    def along(x, axis, mask):
        n = lax.axis_size(axis)
        return lax.ppermute(x, axis, [(s, s ^ mask) for s in range(n)])

    def twin(x):
        return along(x, "expert", 1)

    def chip_exchange(x):
        cut = 2 * cap
        parts = [x[0:cut]]
        for zr in range(1, chips):
            parts.append(along(x[cut * zr : cut * (zr + 1)], "expert", 2 * zr))
        return jnp.concatenate(parts, axis=0)

    mine, me = lax.axis_index("dp"), lax.axis_index("expert")
    idx = jnp.stack([mine, me, me % 2, me // 2]).astype(i32)
    weight_in, weight_out = w_expert_in[0], w_expert_out[0]

    first = me % 2 == 0
    parcel = jnp.concatenate(
        [jnp.where(first, w_query, w_key), jnp.where(first, w_value, w_attn_out)], axis=0
    )
    hx = along(parcel, "dp", 1)
    hy = along(parcel, "dp", 2)

    wr_t, gain_a, gain_b, tab, cot, route_c, seg = lax.optimization_barrier(
        (w_router.T, norm1_gain, norm2_gain, bias_table, cotangent, routes, segments, parcel)
    )[:-1]
    small_own = call(
        "pack", 1, partial(pack_body, experts, smalls), [((smalls, width), bf16)], idx,
        wr_t, gain_a[None], gain_b[None], tab,
    )[0]
    small_x = along(small_own, "dp", 1)
    route_row = route_c.reshape(1, length)
    routes2 = jnp.concatenate([route_row, twin(route_row.astype(f32)).astype(i32)], axis=1)
    r = np.arange(slots)
    consts = np.zeros((slots, 128), np.int32)
    consts[:, 0] = 2 * (r // (2 * cap))
    consts[:, 1] = (r // cap) % 2
    consts[:, 2] = r % cap
    place, g_rows = call(
        "place_cot", 1.5, partial(place_body, experts),
        [((slots, 2 * length), bf16), ((slots, width), bf16)], idx,
        jnp.asarray(consts), routes2, cot, twin(cot),
    )
    seg_c, seg_r = seg.reshape(length, 1), seg.reshape(1, length)
    g_here = chip_exchange(g_rows)
    hx, hy, place, g_here, seg_c, seg_r, route_c, small_own, small_x = lax.optimization_barrier(
        (hx, hy, place, g_here, seg_c, seg_r, route_c, small_own, small_x)
    )
    da = along(jnp.concatenate([hx[0:rows], small_own, small_x], axis=0), "dp", 2)
    db = along(hy[rows:], "dp", 1)
    tx, ty = twin(hx), twin(hy)
    ta, tb = twin(da), twin(db)
    g_here = after(g_here, da, db)
    g_set = [g_here] + [along(g_here, "dp", k) for k in (1, 2, 3)]
    g_back = call("g_back", 2, back_in_body, [((4, slots, width), f32)], idx, weight_out, *g_set)[0]

    w_all, small_all, q, k, v, probs, ctx, mixed, hcat, rp, *left = call(
        "attend", 7, partial(attend_body, experts, smalls, heads),
        [
            ((4, width, width), bf16), ((smalls, width), f32),
            ((length, width), bf16), ((length, width), bf16), ((length, width), bf16),
            ((heads, length, length), f32), ((length, width), bf16), ((length, width), f32),
            ((length, wide), bf16), ((length, experts), f32),
        ]
        + ([((length, width), bf16)] * 4 if chips == 4 else []),
        idx, tokens, seg_c, seg_r, route_c,
        w_query, w_key, w_value, w_attn_out, small_own, small_x, hx, hy, da, db, tx, ty, ta, tb,
    )

    x_rows = call("place_x", 1, place_rows_body, [((slots, wide), bf16)], idx, place, hcat, twin(hcat))[0]
    x_here = chip_exchange(x_rows)
    x_here = after(x_here, *g_set)
    x_set = [x_here] + [along(x_here, "dp", kk) for kk in (1, 2, 3)]
    if chips == 4:
        left = [left[0]] + [along(after(left[zr], x_here), "expert", 2 * zr) for zr in range(1, 4)]
        x_set[3] = after(x_set[3], left[1])
    *d_parts, hid, dpre = call(
        "expert", 4, expert_body,
        [((slots, wide), bf16)] * 4 + [((4, slots, width), bf16)] * 2,
        idx, weight_in, g_back, *x_set,
    )
    d_got = [d_parts[0]] + [along(d_parts[kk], "dp", kk) for kk in (1, 2, 3)]
    y_parts = call("expert_out", 1, expert_out_body, [((slots, width), bf16)] * 4, idx, weight_out, hid)
    grad_in, grad_out = call(
        "expert_grad", 5.5, expert_grad_body,
        [((1, width, weight_in.shape[1]), f32), ((1, weight_out.shape[0], width), f32)], idx,
        hid, dpre, *x_set, *g_set,
    )
    d_here = call("sum_d", 0.7, sum_body, [((slots, wide), bf16)], idx, *d_got)[0]
    y_parts = list(lax.optimization_barrier((*y_parts, d_here))[:-1])
    y_got = [y_parts[0]] + [along(y_parts[kk], "dp", kk) for kk in (1, 2, 3)]
    d_rows = chip_exchange(d_here)
    place_d = after(place, *left) if chips == 4 else place
    back_own, back_other = call(
        "unplace_d", 1, unplace_body, [((length, wide), f32), ((length, wide), bf16)], idx, place_d, d_rows
    )
    back_other = twin(back_other)

    outs = [
        ((length, width), f32), ((4, length, width), bf16), ((experts, width), f32),
        ((1, width), f32), ((heads, 128), f32),
    ]
    if chips == 4:
        outs = outs + [((length, width), bf16)] * 4
    d_mixed, d_all, g_router, g_gain2, g_table, *turned = call(
        "attend_back", 5.5, partial(attend_back_body, experts, heads, chips), outs, idx,
        back_own, back_other, mixed, cotangent, rp, route_c, small_all, w_all, q, k, v, probs, ctx,
        scratch=[pltpu.VMEM((16, 2 * length), f32)],
    )
    d_in = [d_all]
    if chips == 4:
        d_in = [turned[0]] + [along(turned[zr], "expert", 2 * zr) for zr in range(1, 4)]
    d_tokens, small_g, table_g = call(
        "token_grad", 3, partial(token_grad_body, experts, smalls),
        [((length, width), f32), ((smalls, width), bf16), ((smalls, 128), bf16)], idx,
        tokens, d_mixed, d_all, w_all, small_all, g_router, g_gain2, g_table,
    )

    y_got[0] = after(y_got[0], d_mixed)
    y_here = call("sum_y", 0.7, sum_body, [((slots, width), bf16)], idx, *y_got)[0]
    if chips == 4:
        small_s, d_in[1] = lax.optimization_barrier((small_all, d_in[1], small_g, y_here))[0:2]
        keep, send = call(
            "mixer_grad", 2, partial(mixer_grad_body, experts),
            [((width, width // 2), f32), ((width, width // 2), bf16)], idx,
            small_s, *left, *d_in,
            scratch=[pltpu.VMEM((width, width), f32), pltpu.VMEM((4 * length, width), bf16)],
        )
        parts = call(
            "share", 1.2, partial(share_body, shard), [((rows + smalls, width // 2), bf16)] * 4, idx,
            keep, twin(send), small_g, table_g, scratch=[pltpu.VMEM((width, width // 2), f32)],
        )
        got = [parts[0]] + [along(parts[kk], "dp", kk) for kk in (1, 2, 3)]
        total = call("sum_share", 0.7, sum_body, [((rows + smalls, width // 2), bf16)], idx, *got)[0]
        y_here = after(y_here, total)
    y_rows = chip_exchange(y_here)
    y_own, y_other = call(
        "unplace_y", 1, unplace_body, [((length, width), f32), ((length, width), bf16)], idx, place, y_rows
    )
    y_other = twin(y_other)
    gate = jnp.sum(jnp.where(route_c == jnp.arange(experts, dtype=i32)[None, :], rp, 0.0), axis=1, keepdims=True)
    layer_out = (mixed + gate * (y_own + y_other.astype(f32))).astype(bf16)

    if chips == 4:
        a_set = [total] + [along(total, "expert", 2 * zr) for zr in range(1, 4)]
        b_set = [twin(a) for a in a_set]
        g_q, g_k, g_v, g_o, small_t = call(
            "finish", 2, finish_body, [((rows, width), f32)] * 4 + [((smalls, width // 2), f32)], idx, *a_set, *b_set
        )
        r_out = small_t[0:experts, 0:rows].T
        gain1_out = small_t[experts, 0:rows]
        gain2_out = small_t[experts + 1, 0:rows]
        table_out = small_t[experts + 2 : experts + 2 + heads, rows : rows + shard].T
    else:
        gain1 = small_all[experts : experts + 1]
        x = tokens.astype(f32)
        h1 = (x * rms_scale(x) * gain1).astype(bf16)
        both = jnp.concatenate(
            [tn(h1, d_all[0]), tn(h1, d_all[1]), tn(h1, d_all[2]), tn(ctx, d_all[3]), small_g.T.astype(f32)], axis=1
        )
        both = lax.psum_scatter(both, "dp", scatter_dimension=0, tiled=True)
        both = lax.psum(both, "expert")
        g_q, g_k, g_v, g_o = (both[:, m * width : (m + 1) * width] for m in range(4))
        rest = both[:, 4 * width :]
        r_out = rest[:, 0:experts]
        gain1_out, gain2_out = rest[:, experts], rest[:, experts + 1]
        tab_g = table_g.T[0 : 4 * shard, experts + 2 : experts + 2 + heads].astype(f32)
        table_out = lax.psum(lax.psum_scatter(tab_g, "dp", scatter_dimension=0, tiled=True), "expert")
    return (
        layer_out, d_tokens, g_q, g_k, g_v, g_o, r_out, gain1_out, gain2_out, table_out, grad_in, grad_out,
    )


def solution(mesh):
    return jax.shard_map(
        on_device,
        mesh=mesh,
        in_specs=(
            P(("dp", "expert"), None),
            P("dp", None),
            P("dp", None),
            P("dp", None),
            P("dp", None),
            P("dp", None),
            P("dp"),
            P("dp"),
            P("dp", None),
            P("expert", None, "dp"),
            P("expert", "dp", None),
            P(("dp", "expert"), None),
            P(("dp", "expert")),
            P(("dp", "expert"), None),
        ),
        out_specs=(
            P(("dp", "expert"), None),
            P(("dp", "expert"), None),
            P("dp", None),
            P("dp", None),
            P("dp", None),
            P("dp", None),
            P("dp", None),
            P("dp"),
            P("dp"),
            P("dp", None),
            P("expert", None, "dp"),
            P("expert", "dp", None),
        ),
        check_vma=False,
    )
```

```python
from functools import partial

import jax
import jax.numpy as jnp
import numpy as np
from jax import lax
from jax.experimental import pallas as pl
from jax.experimental.pallas import tpu as pltpu
from jax.sharding import PartitionSpec as P

eps = 1e-06
bucket_edges = (12, 16, 23, 32, 46, 64, 91)
f32 = jnp.float32
bf16 = jnp.bfloat16
i32 = jnp.int32
gelu_a = float(np.sqrt(2.0 / np.pi))
gelu_b = 0.044715

owner_of = (1, 2, 0, 3)


def nn(left, right):
    return lax.dot_general(left, right, (((1,), (0,)), ((), ())), preferred_element_type=f32)


def nt(left, right):
    return lax.dot_general(left, right, (((1,), (1,)), ((), ())), preferred_element_type=f32)


def tn(left, right):
    return lax.dot_general(left, right, (((0,), (0,)), ((), ())), preferred_element_type=f32)


def iota(shape, dim):
    return lax.broadcasted_iota(i32, shape, dim)


def after(value, *earlier):
    return lax.optimization_barrier((value, *earlier))[0]


def call(name, micros, body, outs, idx, *args, scratch=()):
    return pl.pallas_call(
        body,
        name=name,
        cost_estimate=pl.CostEstimate(flops=int(micros * 1.1e9), bytes_accessed=int(micros * 1e6), transcendentals=0),
        out_shape=[jax.ShapeDtypeStruct(s, d) for s, d in outs],
        in_specs=[pl.BlockSpec(memory_space=pltpu.SMEM)]
        + [pl.BlockSpec(memory_space=pltpu.VMEM)] * len(args),
        out_specs=[pl.BlockSpec(memory_space=pltpu.VMEM)] * len(outs),
        scratch_shapes=list(scratch),
        compiler_params=pltpu.CompilerParams(vmem_limit_bytes=40 * 1024 * 1024),
    )(idx, *args)


def rms_scale(values):
    return lax.rsqrt(jnp.mean(values * values, axis=-1, keepdims=True) + eps)


def norm_back(d_normed, normed, scale):
    return scale * (d_normed - normed * jnp.mean(d_normed * normed, axis=-1, keepdims=True))


def bucket_onehot(rows, length, centred):
    col = iota((rows, 2 * length), 1)
    n = (length - 1) - col if centred else jnp.where(col < length, -col, 2 * length - col)
    mag = jnp.abs(n)
    far = jnp.full_like(mag, 8)
    for threshold in bucket_edges:
        far = far + (mag >= threshold).astype(i32)
    bucket = jnp.where(n < 0, 16, 0) + jnp.where(mag < 8, mag, far)
    return (bucket == iota((rows, 2 * length), 0)).astype(f32).astype(bf16)


def pack_body(experts, smalls, idx, wr_t, g1, g2, tab, out):
    rows = wr_t.shape[1]
    heads, shard = tab.shape[1], tab.shape[0]
    pick = (iota((smalls, experts), 0) == iota((smalls, experts), 1)).astype(f32).astype(bf16)
    part = nn(pick, wr_t[...])
    line = iota((smalls, rows), 0)
    part = part + jnp.where(line == experts, g1[...].astype(f32), 0.0)
    part = part + jnp.where(line == experts + 1, g2[...].astype(f32), 0.0)
    width = out.shape[1]
    spread = (iota((rows, width), 0) == iota((rows, width), 1)).astype(f32).astype(bf16)
    whole = nn(part.astype(bf16), spread)
    pick_t = (iota((smalls, heads), 0) == iota((smalls, heads), 1) + experts + 2).astype(f32)
    table_t = nt(pick_t.astype(bf16), tab[...])
    spread_t = (iota((shard, width), 0) + rows == iota((shard, width), 1)).astype(f32)
    whole = whole + nn(table_t.astype(bf16), spread_t.astype(bf16))
    out[...] = whole.astype(bf16)


def place_body(experts, idx, consts, routes2, cot, cot_t, place, rows_out):
    me = idx[1]
    slots = place.shape[0]
    both = routes2.shape[1]
    half = both // 2
    route = routes2[...]
    hot = (iota((experts, both), 0) == route).astype(f32)
    a, b = iota((both, both), 0), iota((both, both), 1)
    earlier = ((a < b) & ((a < half) == (b < half))).astype(f32).astype(bf16)
    ranks = nn(hot.astype(bf16), earlier)
    slot = jnp.sum(hot * ranks, axis=0, keepdims=True).astype(i32)
    which = consts[:, 0:1] ^ me
    turn = consts[:, 1:2]
    number = consts[:, 2:3]
    side = (iota((slots, both), 1) >= half).astype(i32)
    hit = (which == route) & (number == slot) & (turn == side)
    placer = hit.astype(f32).astype(bf16)
    place[...] = placer
    rows = nn(placer[:, 0:half], cot[...]) + nn(placer[:, half:both], cot_t[...])
    rows_out[...] = rows.astype(bf16)


def place_rows_body(idx, place, own, other, rows_out):
    half = own.shape[0]
    rows = nn(place[:, 0:half], own[...]) + nn(place[:, half : 2 * half], other[...])
    rows_out[...] = rows.astype(bf16)


def unplace_body(idx, place, rows, own, other):
    half = own.shape[0]
    arrived = rows[...]
    own[...] = tn(place[:, 0:half], arrived)
    other[...] = tn(place[:, half : 2 * half], arrived).astype(bf16)


def attend_body(
    experts, smalls, heads, idx,
    tokens, seg_c, seg_r, routes_c, wq, wk, wv, wo, s0, s1, hx, hy, da, db, tx, ty, ta, tb,
    w_all, small_all, q_o, k_o, v_o, probs_o, ctx_o, mixed_o, hcat_o, rp_o, *left,
):
    mine, core = idx[0], idx[2]
    rows, width = wq.shape
    length = tokens.shape[0]
    size = width // heads
    home = pl.multiple_of(mine * rows, 64)
    for m, w in enumerate((wq, wk, wv, wo)):
        w_all[m, pl.ds(home, rows), :] = w[...]
    for k, piece, held in ((1, hx, core), (2, hy, core), (1, tx, 1 - core), (2, ty, 1 - core)):
        at = pl.multiple_of((mine ^ k) * rows, 64)
        w_all[held, pl.ds(at, rows), :] = piece[0:rows, :]
        w_all[2 + held, pl.ds(at, rows), :] = piece[rows : 2 * rows, :]
    at = pl.multiple_of((mine ^ 3) * rows, 64)
    for first, second, held in ((da, db, core), (ta, tb, 1 - core)):
        w_all[held, pl.ds(at, rows), :] = first[0:rows, :]
        w_all[2 + held, pl.ds(at, rows), :] = second[...]
    small = jnp.zeros((smalls, width), f32)
    table_t = jnp.zeros((smalls, 128), f32)
    shard = 32 // 4
    for k, part in (
        (0, s0[...]), (1, s1[...]), (2, da[rows : rows + smalls, 0:256]), (3, da[rows : rows + smalls, 256:512])
    ):
        j = mine ^ k
        r, c = iota((256, width), 0), iota((256, width), 1)
        small = small + nn(part, ((r < rows) & (c == r + rows * j)).astype(f32).astype(bf16))
        r, c = iota((256, 128), 0), iota((256, 128), 1)
        keep = (r >= rows) & (r < rows + shard) & (c == r - rows + shard * j)
        table_t = table_t + nn(part, keep.astype(f32).astype(bf16))
    small_all[...] = small
    gain1 = small[experts : experts + 1, :]
    gain2 = small[experts + 1 : experts + 2, :]
    per_offset = nn(table_t.astype(bf16), bucket_onehot(128, length, False))

    x = tokens[...].astype(f32)
    h1 = (x * rms_scale(x) * gain1).astype(bf16)
    q_o[...] = nn(h1, w_all[0]).astype(bf16)
    k_o[...] = nn(h1, w_all[1]).astype(bf16)
    v_o[...] = nn(h1, w_all[2]).astype(bf16)
    same = seg_c[...] == seg_r[...]
    low = iota((length, 2 * size), 1) < size
    zero = jnp.zeros((length, 2 * size), bf16)
    for p in range(heads // 2):
        cols = slice(2 * size * p, 2 * size * (p + 1))
        q2, k2, v2 = q_o[:, cols], k_o[:, cols], v_o[:, cols]
        got = []
        for t in range(2):
            h = 2 * p + t
            qh = jnp.where(low, q2, zero) if t == 0 else jnp.where(low, zero, q2)
            line = per_offset[experts + 2 + h : experts + 3 + h, :]
            bias = pltpu.roll(
                jnp.broadcast_to(line, (length, 2 * length)), 0, 1, stride=1, stride_axis=0
            )[:, 0:length]
            s = jnp.where(same, nt(qh, k2) + bias, -1000000000.0)
            e = jnp.exp(s - jnp.max(s, axis=-1, keepdims=True))
            pr = e / jnp.sum(e, axis=-1, keepdims=True)
            probs_o[h] = pr
            got.append(nn(pr.astype(bf16), v2))
        ctx_o[:, cols] = jnp.where(low, got[0], got[1]).astype(bf16)
    mixed = x + nn(ctx_o[...], w_all[3])
    mixed_o[...] = mixed
    h2 = (mixed * rms_scale(mixed) * gain2).astype(bf16)
    logits = nt(h2, small[0:experts, :].astype(bf16))
    e = jnp.exp(logits - jnp.max(logits, axis=-1, keepdims=True))
    rp = e / jnp.sum(e, axis=-1, keepdims=True)
    rp_o[...] = rp
    gate = jnp.sum(jnp.where(routes_c[...] == iota((length, experts), 1), rp, 0.0), axis=-1, keepdims=True)
    hcat_o[:, 0:width] = h2
    high = gate.astype(bf16).astype(f32)
    lane = iota((length, 128), 1)
    tail = jnp.where(lane == 0, high, jnp.where(lane == 1, gate - high, 0.0))
    hcat_o[:, width : width + 128] = tail.astype(bf16)
    for zr, item in enumerate(left):

        @pl.when((idx[3] ^ zr) == owner_of[3])
        def _():
            item[...] = ctx_o[...]

        @pl.when((idx[3] ^ zr) != owner_of[3])
        def _():
            item[...] = tokens[...]


def back_in_body(idx, w_out, *refs):
    for k in range(4):
        refs[4][k] = nt(refs[k][...], w_out[...])


def expert_body(idx, w_in, g_all, x0, x1, x2, x3, y0, y1, y2, y3, hid_o, dpre_o):
    width = w_in.shape[0]
    lane = iota((x0.shape[0], 128), 1)
    for k, (x, y) in enumerate(((x0, y0), (x1, y1), (x2, y2), (x3, y3))):
        pre = nn(x[:, 0:width], w_in[...])
        tail = x[:, width : width + 128].astype(f32)
        gate = jnp.sum(jnp.where(lane < 2, tail, 0.0), axis=-1, keepdims=True)
        sq = pre * pre
        t = jnp.tanh(gelu_a * (pre + gelu_b * sq * pre))
        hid = (0.5 * pre * (1.0 + t)).astype(bf16)
        slope = 0.5 * (1.0 + t) + 0.5 * pre * (1.0 - t * t) * (gelu_a * (1.0 + 3.0 * gelu_b * sq))
        g = g_all[k]
        dpre = (gate * g * slope).astype(bf16)
        hid_o[k] = hid
        dpre_o[k] = dpre
        d_gate = jnp.sum(hid.astype(f32) * g, axis=-1, keepdims=True)
        y[:, 0:width] = nt(dpre, w_in[...]).astype(bf16)
        y[:, width : width + 128] = jnp.where(lane == 0, d_gate, 0.0).astype(bf16)


def expert_out_body(idx, w_out, hid, y0, y1, y2, y3):
    for k, y in enumerate((y0, y1, y2, y3)):
        y[...] = nn(hid[k], w_out[...]).astype(bf16)


def expert_grad_body(idx, hid, dpre, x0, x1, x2, x3, g0, g1, g2, g3, gi, go):
    width = gi.shape[1]
    lane = iota((x0.shape[0], 128), 1)
    acc_i = jnp.zeros((width, dpre.shape[2]), f32)
    for k, x in enumerate((x0, x1, x2, x3)):
        acc_i = acc_i + tn(x[:, 0:width], dpre[k])
    gi[0] = acc_i
    acc_o = jnp.zeros((hid.shape[2], width), f32)
    for k, (x, g) in enumerate(((x0, g0), (x1, g1), (x2, g2), (x3, g3))):
        tail = x[:, width : width + 128].astype(f32)
        gate = jnp.sum(jnp.where(lane < 2, tail, 0.0), axis=-1, keepdims=True)
        acc_o = acc_o + tn(hid[k], (gate * g[...].astype(f32)).astype(bf16))
    go[0] = acc_o


def attend_back_body(
    experts, heads, chips, idx,
    own, other, mixed_r, cot, rp_r, routes_c, small_all, w_all, q, k, v, probs, ctx,
    dmixed_o, d_o, router_o, gain2_o, table_o, *rest,
):
    turned, diag = rest[:-1], rest[-1]
    length, width = mixed_r.shape
    size = width // heads
    back = own[...] + other[...].astype(f32)
    lane = iota((length, 128), 1)
    d_gate = jnp.sum(jnp.where(lane == 0, back[:, width : width + 128], 0.0), axis=-1, keepdims=True)
    hot = (routes_c[...] == iota((length, experts), 1)).astype(f32)
    rp = rp_r[...]
    gate = jnp.sum(rp * hot, axis=-1, keepdims=True)
    d_logits = (rp * (hot - gate) * d_gate).astype(bf16)
    gain2 = small_all[experts + 1 : experts + 2, :]
    wr_t = small_all[0:experts, :].astype(bf16)
    mixed = mixed_r[...]
    scale2 = rms_scale(mixed)
    normed2 = mixed * scale2
    h2 = (normed2 * gain2).astype(bf16)
    router_o[...] = tn(d_logits, h2)
    d_h2 = nn(d_logits, wr_t) + back[:, 0:width]
    gain2_o[...] = jnp.sum(d_h2 * normed2, axis=0, keepdims=True)
    d_mixed = cot[...].astype(f32) + norm_back(d_h2 * gain2, normed2, scale2)
    dmixed_o[...] = d_mixed
    d_attn = d_mixed.astype(bf16)
    d_o[3] = d_attn
    d_ctx = nt(d_attn, w_all[3]).astype(bf16)
    low = iota((length, 2 * size), 1) < size
    zero = jnp.zeros((length, 2 * size), bf16)
    blank = jnp.zeros((length, length), f32)
    upside = iota((length, length), 0) + iota((length, length), 1) == length - 1
    upside = upside.astype(f32).astype(bf16)
    for p in range(heads // 2):
        cols = slice(2 * size * p, 2 * size * (p + 1))
        q2, k2, v2, c2 = q[:, cols], k[:, cols], v[:, cols], d_ctx[:, cols]
        gq, gk, gv = [], [], []
        for t in range(2):
            h = 2 * p + t
            ch = jnp.where(low, c2, zero) if t == 0 else jnp.where(low, zero, c2)
            pr = probs[h]
            dw = nt(ch, v2)
            gv.append(tn(pr.astype(bf16), c2))
            ds = (pr * (dw - jnp.sum(pr * dw, axis=-1, keepdims=True))).astype(bf16)
            gq.append(nn(ds, k2))
            gk.append(tn(ds, q2))
            wide = jnp.concatenate([nn(upside, ds), blank], axis=1)
            wide = pltpu.roll(wide, 0, 1, stride=1, stride_axis=0)
            diag[h : h + 1, :] = jnp.sum(wide, axis=0, keepdims=True)
        d_o[0, :, cols] = jnp.where(low, gq[0], gq[1]).astype(bf16)
        d_o[1, :, cols] = jnp.where(low, gk[0], gk[1]).astype(bf16)
        d_o[2, :, cols] = jnp.where(low, gv[0], gv[1]).astype(bf16)
    sums = diag[0:heads, :]
    onehot = bucket_onehot(128, length, True)
    high = sums.astype(bf16)
    mid = (sums - high.astype(f32)).astype(bf16)
    table_o[...] = nt(high, onehot) + nt(mid, onehot)
    if chips == 4:
        z = idx[3]
        for zr in range(4):
            dest = z ^ zr
            for m in range(4):

                @pl.when(dest == owner_of[m])
                def _():
                    turned[zr][...] = d_o[m]


def token_grad_body(experts, smalls, idx, tokens, dmixed, d, w_all, small_all, router, gain2, table, dtok_o, small_o, table_o):
    x = tokens[...].astype(f32)
    scale1 = rms_scale(x)
    normed1 = x * scale1
    gain1 = small_all[experts : experts + 1, :]
    d_h1 = nt(d[0], w_all[0]) + nt(d[1], w_all[1]) + nt(d[2], w_all[2])
    g_gain1 = jnp.sum(d_h1 * normed1, axis=0, keepdims=True)
    dtok_o[...] = dmixed[...] + norm_back(d_h1 * gain1, normed1, scale1)
    width = x.shape[1]
    pick = (iota((smalls, experts), 0) == iota((smalls, experts), 1)).astype(f32).astype(bf16)
    line = iota((smalls, width), 0)
    out = nn(pick, router[...].astype(bf16))
    out = out + jnp.where(line == experts, g_gain1, 0.0) + jnp.where(line == experts + 1, gain2[...], 0.0)
    small_o[...] = out.astype(bf16)
    heads = table.shape[0]
    pick_t = (iota((smalls, heads), 0) == iota((smalls, heads), 1) + experts + 2).astype(f32)
    table_o[...] = nn(pick_t.astype(bf16), table[...].astype(bf16)).astype(bf16)


def mixer_grad_body(experts, idx, small_all, l0, l1, l2, l3, d0, d1, d2, d3, keep, send, acc, left):
    z, core = idx[3], idx[2]
    gain1 = small_all[experts : experts + 1, :]
    rows = l0.shape[0]

    @pl.when(z == owner_of[3])
    def _():
        for n, c in enumerate((l0, l1, l2, l3)):
            left[n * rows : (n + 1) * rows, :] = c[...]

    @pl.when(z != owner_of[3])
    def _():
        for n, item in enumerate((l0, l1, l2, l3)):
            x = item[...].astype(f32)
            left[n * rows : (n + 1) * rows, :] = (x * rms_scale(x) * gain1).astype(bf16)

    right = jnp.concatenate([d0[...], d1[...], d2[...], d3[...]], axis=0)
    acc[...] = tn(left[...], right)
    half = keep.shape[1]
    keep[...] = acc[:, pl.ds(pl.multiple_of(core * half, 128), half)]
    send[...] = acc[:, pl.ds(pl.multiple_of((1 - core) * half, 128), half)].astype(bf16)


def share_body(shard, idx, keep, got, small, table, s0, s1, s2, s3, total):
    mine = idx[0]
    total[...] = keep[...] + got[...].astype(f32)
    half = keep.shape[1]
    rows = total.shape[0] // 4
    width = small.shape[1]
    for k, out in enumerate((s0, s1, s2, s3)):
        j = mine ^ k
        out[0:rows, :] = total[pl.ds(pl.multiple_of(j * rows, 64), rows), :].astype(bf16)
        r, c = iota((width, half), 0), iota((width, half), 1)
        part = nn(small[...], ((c < rows) & (r == c + rows * j)).astype(f32).astype(bf16))
        r, c = iota((128, half), 0), iota((128, half), 1)
        keep_t = (c >= rows) & (c < rows + shard) & (r == c - rows + shard * j)
        part = part + nn(table[...], keep_t.astype(f32).astype(bf16))
        out[rows : rows + small.shape[0], :] = part.astype(bf16)


def sum_body(idx, a, b, c, d, out):
    out[...] = (
        a[...].astype(f32) + b[...].astype(f32) + c[...].astype(f32) + d[...].astype(f32)
    ).astype(bf16)


def finish_body(idx, a0, a1, a2, a3, b0, b1, b2, b3, gq, gk, gv, go, small):
    z, core = idx[3], idx[2]
    half = a0.shape[1]
    rows = gq.shape[0]
    at = pl.multiple_of(core * half, 128)
    off = pl.multiple_of((1 - core) * half, 128)
    for m, out in enumerate((gq, gk, gv, go)):
        for zr, (a, b) in enumerate(((a0, b0), (a1, b1), (a2, b2), (a3, b3))):

            @pl.when((z ^ zr) == owner_of[m])
            def _():
                out[:, pl.ds(at, half)] = a[0:rows, :].astype(f32)
                out[:, pl.ds(off, half)] = b[0:rows, :].astype(f32)

    total = jnp.zeros(small.shape, f32)
    for item in (a0, a1, a2, a3, b0, b1, b2, b3):
        total = total + item[rows : rows + small.shape[0], :].astype(f32)
    small[...] = total


def on_device(
    tokens, w_query, w_key, w_value, w_attn_out, w_router, norm1_gain, norm2_gain, bias_table,
    w_expert_in, w_expert_out, routes, segments, cotangent,
):
    experts = lax.axis_size("expert")
    chips = experts // 2
    length, width = tokens.shape
    heads = bias_table.shape[1]
    rows = w_query.shape[0]
    shard = bias_table.shape[0]
    cap = 5 * length // (4 * experts)
    smalls = -(-(experts + 2 + heads) // 16) * 16
    slots = experts * cap
    wide = width + 128

    def along(x, axis, mask):
        n = lax.axis_size(axis)
        return lax.ppermute(x, axis, [(s, s ^ mask) for s in range(n)])

    def twin(x):
        return along(x, "expert", 1)

    def chip_exchange(x):
        cut = 2 * cap
        parts = [x[0:cut]]
        for zr in range(1, chips):
            parts.append(along(x[cut * zr : cut * (zr + 1)], "expert", 2 * zr))
        return jnp.concatenate(parts, axis=0)

    mine, me = lax.axis_index("dp"), lax.axis_index("expert")
    idx = jnp.stack([mine, me, me % 2, me // 2]).astype(i32)
    weight_in, weight_out = w_expert_in[0], w_expert_out[0]

    first = me % 2 == 0
    parcel = jnp.concatenate(
        [jnp.where(first, w_query, w_key), jnp.where(first, w_value, w_attn_out)], axis=0
    )
    hx = along(parcel, "dp", 1)
    hy = along(parcel, "dp", 2)

    wr_t, gain_a, gain_b, tab, cot, route_c, seg = lax.optimization_barrier(
        (w_router.T, norm1_gain, norm2_gain, bias_table, cotangent, routes, segments, parcel)
    )[:-1]
    small_own = call(
        "pack", 1, partial(pack_body, experts, smalls), [((smalls, 256), bf16)], idx,
        wr_t, gain_a[None], gain_b[None], tab,
    )[0]
    small_x = along(small_own, "dp", 1)
    route_row = route_c.reshape(1, length)
    routes2 = jnp.concatenate([route_row, twin(route_row.astype(f32)).astype(i32)], axis=1)
    r = np.arange(slots)
    consts = np.zeros((slots, 128), np.int32)
    consts[:, 0] = 2 * (r // (2 * cap))
    consts[:, 1] = (r // cap) % 2
    consts[:, 2] = r % cap
    place, g_rows = call(
        "place_cot", 1.5, partial(place_body, experts),
        [((slots, 2 * length), bf16), ((slots, width), bf16)], idx,
        jnp.asarray(consts), routes2, cot, twin(cot),
    )
    seg_c, seg_r = seg.reshape(length, 1), seg.reshape(1, length)
    g_here = chip_exchange(g_rows)
    hx, hy, place, g_here, seg_c, seg_r, route_c, small_own, small_x = lax.optimization_barrier(
        (hx, hy, place, g_here, seg_c, seg_r, route_c, small_own, small_x)
    )
    tail = jnp.zeros((smalls, width - 512), bf16)
    tail = jnp.concatenate([small_own, small_x, tail], axis=1)
    da = along(jnp.concatenate([hx[0:rows], tail], axis=0), "dp", 2)
    db = along(hy[rows:], "dp", 1)
    tx, ty = twin(hx), twin(hy)
    ta, tb = twin(da), twin(db)
    g_here = after(g_here, da, db)
    g_set = [g_here] + [along(g_here, "dp", k) for k in (1, 2, 3)]
    g_back = call("g_back", 2, back_in_body, [((4, slots, width), f32)], idx, weight_out, *g_set)[0]

    w_all, small_all, q, k, v, probs, ctx, mixed, hcat, rp, *left = call(
        "attend", 7, partial(attend_body, experts, smalls, heads),
        [
            ((4, width, width), bf16), ((smalls, width), f32),
            ((length, width), bf16), ((length, width), bf16), ((length, width), bf16),
            ((heads, length, length), f32), ((length, width), bf16), ((length, width), f32),
            ((length, wide), bf16), ((length, experts), f32),
        ]
        + ([((length, width), bf16)] * 4 if chips == 4 else []),
        idx, tokens, seg_c, seg_r, route_c,
        w_query, w_key, w_value, w_attn_out, small_own, small_x, hx, hy, da, db, tx, ty, ta, tb,
    )

    x_rows = call("place_x", 1, place_rows_body, [((slots, wide), bf16)], idx, place, hcat, twin(hcat))[0]
    x_here = chip_exchange(x_rows)
    x_set = [x_here] + [along(x_here, "dp", kk) for kk in (1, 2, 3)]
    if chips == 4:
        left = [left[0]] + [along(after(left[zr], x_here), "expert", 2 * zr) for zr in range(1, 4)]
        x_set[3] = after(x_set[3], left[1], left[2])
    *d_parts, hid, dpre = call(
        "expert", 4, expert_body,
        [((slots, wide), bf16)] * 4 + [((4, slots, width), bf16)] * 2,
        idx, weight_in, g_back, *x_set,
    )
    d_got = [d_parts[0]] + [along(d_parts[kk], "dp", kk) for kk in (1, 2, 3)]
    y_parts = call("expert_out", 1, expert_out_body, [((slots, width), bf16)] * 4, idx, weight_out, hid)
    grad_in, grad_out = call(
        "expert_grad", 5.5, expert_grad_body,
        [((1, width, weight_in.shape[1]), f32), ((1, weight_out.shape[0], width), f32)], idx,
        hid, dpre, *x_set, *g_set,
    )
    d_here = call("sum_d", 0.7, sum_body, [((slots, wide), bf16)], idx, *d_got)[0]
    y_parts = list(lax.optimization_barrier((*y_parts, d_here))[:-1])
    y_got = [y_parts[0]] + [along(y_parts[kk], "dp", kk) for kk in (1, 2, 3)]
    d_rows = chip_exchange(d_here)
    place_d = after(place, *left) if chips == 4 else place
    back_own, back_other = call(
        "unplace_d", 1, unplace_body, [((length, wide), f32), ((length, wide), bf16)], idx, place_d, d_rows
    )
    back_other = twin(back_other)

    outs = [
        ((length, width), f32), ((4, length, width), bf16), ((experts, width), f32),
        ((1, width), f32), ((heads, 128), f32),
    ]
    if chips == 4:
        outs = outs + [((length, width), bf16)] * 4
    d_mixed, d_all, g_router, g_gain2, g_table, *turned = call(
        "attend_back", 5.5, partial(attend_back_body, experts, heads, chips), outs, idx,
        back_own, back_other, mixed, cotangent, rp, route_c, small_all, w_all, q, k, v, probs, ctx,
        scratch=[pltpu.VMEM((16, 2 * length), f32)],
    )
    d_in = [d_all]
    if chips == 4:
        d_in = [turned[0]] + [along(turned[zr], "expert", 2 * zr) for zr in range(1, 4)]
    d_tokens, small_g, table_g = call(
        "token_grad", 3, partial(token_grad_body, experts, smalls),
        [((length, width), f32), ((smalls, width), bf16), ((smalls, 128), bf16)], idx,
        tokens, d_mixed, d_all, w_all, small_all, g_router, g_gain2, g_table,
    )

    y_got[0] = after(y_got[0], d_mixed)
    y_here = call("sum_y", 0.7, sum_body, [((slots, width), bf16)], idx, *y_got)[0]
    if chips == 4:
        small_s, d_in[1] = lax.optimization_barrier((small_all, d_in[1], small_g, y_here))[0:2]
        keep, send = call(
            "mixer_grad", 2, partial(mixer_grad_body, experts),
            [((width, width // 2), f32), ((width, width // 2), bf16)], idx,
            small_s, *left, *d_in,
            scratch=[pltpu.VMEM((width, width), f32), pltpu.VMEM((4 * length, width), bf16)],
        )
        parts = call(
            "share", 1.2, partial(share_body, shard), [((rows + smalls, width // 2), bf16)] * 4, idx,
            keep, twin(send), small_g, table_g, scratch=[pltpu.VMEM((width, width // 2), f32)],
        )
        got = [parts[0]] + [along(parts[kk], "dp", kk) for kk in (1, 2, 3)]
        total = call("sum_share", 0.7, sum_body, [((rows + smalls, width // 2), bf16)], idx, *got)[0]
        y_here = after(y_here, total)
    y_rows = chip_exchange(y_here)
    y_own, y_other = call(
        "unplace_y", 1, unplace_body, [((length, width), f32), ((length, width), bf16)], idx, place, y_rows
    )
    y_other = twin(y_other)
    gate = jnp.sum(jnp.where(route_c == jnp.arange(experts, dtype=i32)[None, :], rp, 0.0), axis=1, keepdims=True)
    layer_out = (mixed + gate * (y_own + y_other.astype(f32))).astype(bf16)

    if chips == 4:
        a_set = [total] + [along(total, "expert", 2 * zr) for zr in range(1, 4)]
        b_set = [twin(a) for a in a_set]
        g_q, g_k, g_v, g_o, small_t = call(
            "finish", 2, finish_body, [((rows, width), f32)] * 4 + [((smalls, width // 2), f32)], idx, *a_set, *b_set
        )
        r_out = small_t[0:experts, 0:rows].T
        gain1_out = small_t[experts, 0:rows]
        gain2_out = small_t[experts + 1, 0:rows]
        table_out = small_t[experts + 2 : experts + 2 + heads, rows : rows + shard].T
    else:
        gain1 = small_all[experts : experts + 1]
        x = tokens.astype(f32)
        h1 = (x * rms_scale(x) * gain1).astype(bf16)
        both = jnp.concatenate(
            [tn(h1, d_all[0]), tn(h1, d_all[1]), tn(h1, d_all[2]), tn(ctx, d_all[3]), small_g.T.astype(f32)], axis=1
        )
        both = lax.psum_scatter(both, "dp", scatter_dimension=0, tiled=True)
        both = lax.psum(both, "expert")
        g_q, g_k, g_v, g_o = (both[:, m * width : (m + 1) * width] for m in range(4))
        rest = both[:, 4 * width :]
        r_out = rest[:, 0:experts]
        gain1_out, gain2_out = rest[:, experts], rest[:, experts + 1]
        tab_g = table_g.T[0 : 4 * shard, experts + 2 : experts + 2 + heads].astype(f32)
        table_out = lax.psum(lax.psum_scatter(tab_g, "dp", scatter_dimension=0, tiled=True), "expert")
    return (
        layer_out, d_tokens, g_q, g_k, g_v, g_o, r_out, gain1_out, gain2_out, table_out, grad_in, grad_out,
    )


def solution(mesh):
    return jax.shard_map(
        on_device,
        mesh=mesh,
        in_specs=(
            P(("dp", "expert"), None),
            P("dp", None),
            P("dp", None),
            P("dp", None),
            P("dp", None),
            P("dp", None),
            P("dp"),
            P("dp"),
            P("dp", None),
            P("expert", None, "dp"),
            P("expert", "dp", None),
            P(("dp", "expert"), None),
            P(("dp", "expert")),
            P(("dp", "expert"), None),
        ),
        out_specs=(
            P(("dp", "expert"), None),
            P(("dp", "expert"), None),
            P("dp", None),
            P("dp", None),
            P("dp", None),
            P("dp", None),
            P("dp", None),
            P("dp"),
            P("dp"),
            P("dp", None),
            P("expert", None, "dp"),
            P("expert", "dp", None),
        ),
        check_vma=False,
    )
```

```python
from functools import partial

import jax
import jax.numpy as jnp
import numpy as np
from jax import lax
from jax.experimental import pallas as pl
from jax.experimental.pallas import tpu as pltpu
from jax.sharding import PartitionSpec as P

eps = 1e-06
bucket_edges = (12, 16, 23, 32, 46, 64, 91)
f32 = jnp.float32
bf16 = jnp.bfloat16
i32 = jnp.int32
gelu_a = float(np.sqrt(2.0 / np.pi))
gelu_b = 0.044715

owner_of = (1, 2, 0, 3)


def nn(left, right):
    return lax.dot_general(left, right, (((1,), (0,)), ((), ())), preferred_element_type=f32)


def nt(left, right):
    return lax.dot_general(left, right, (((1,), (1,)), ((), ())), preferred_element_type=f32)


def tn(left, right):
    return lax.dot_general(left, right, (((0,), (0,)), ((), ())), preferred_element_type=f32)


def iota(shape, dim):
    return lax.broadcasted_iota(i32, shape, dim)


def after(value, *earlier):
    return lax.optimization_barrier((value, *earlier))[0]


def call(name, micros, body, outs, idx, *args, scratch=()):
    return pl.pallas_call(
        body,
        name=name,
        cost_estimate=pl.CostEstimate(flops=int(micros * 1.1e9), bytes_accessed=int(micros * 1e6), transcendentals=0),
        out_shape=[jax.ShapeDtypeStruct(s, d) for s, d in outs],
        in_specs=[pl.BlockSpec(memory_space=pltpu.SMEM)]
        + [pl.BlockSpec(memory_space=pltpu.VMEM)] * len(args),
        out_specs=[pl.BlockSpec(memory_space=pltpu.VMEM)] * len(outs),
        scratch_shapes=list(scratch),
        compiler_params=pltpu.CompilerParams(vmem_limit_bytes=40 * 1024 * 1024),
    )(idx, *args)


def rms_scale(values):
    return lax.rsqrt(jnp.mean(values * values, axis=-1, keepdims=True) + eps)


def norm_back(d_normed, normed, scale):
    return scale * (d_normed - normed * jnp.mean(d_normed * normed, axis=-1, keepdims=True))


def bucket_onehot(rows, length, centred):
    col = iota((rows, 2 * length), 1)
    n = (length - 1) - col if centred else jnp.where(col < length, -col, 2 * length - col)
    mag = jnp.abs(n)
    far = jnp.full_like(mag, 8)
    for threshold in bucket_edges:
        far = far + (mag >= threshold).astype(i32)
    bucket = jnp.where(n < 0, 16, 0) + jnp.where(mag < 8, mag, far)
    return (bucket == iota((rows, 2 * length), 0)).astype(f32).astype(bf16)


def pack_body(experts, smalls, idx, wr_t, g1, g2, tab, out):
    rows = wr_t.shape[1]
    heads, shard = tab.shape[1], tab.shape[0]
    pick = (iota((smalls, experts), 0) == iota((smalls, experts), 1)).astype(f32).astype(bf16)
    part = nn(pick, wr_t[...])
    line = iota((smalls, rows), 0)
    part = part + jnp.where(line == experts, g1[...].astype(f32), 0.0)
    part = part + jnp.where(line == experts + 1, g2[...].astype(f32), 0.0)
    width = out.shape[1]
    spread = (iota((rows, width), 0) == iota((rows, width), 1)).astype(f32).astype(bf16)
    whole = nn(part.astype(bf16), spread)
    pick_t = (iota((smalls, heads), 0) == iota((smalls, heads), 1) + experts + 2).astype(f32)
    table_t = nt(pick_t.astype(bf16), tab[...])
    spread_t = (iota((shard, width), 0) + rows == iota((shard, width), 1)).astype(f32)
    whole = whole + nn(table_t.astype(bf16), spread_t.astype(bf16))
    out[...] = whole.astype(bf16)


def place_body(experts, idx, consts, routes2, cot, cot_t, place, rows_out):
    me = idx[1]
    slots = place.shape[0]
    both = routes2.shape[1]
    half = both // 2
    route = routes2[...]
    hot = (iota((experts, both), 0) == route).astype(f32)
    a, b = iota((both, both), 0), iota((both, both), 1)
    earlier = ((a < b) & ((a < half) == (b < half))).astype(f32).astype(bf16)
    ranks = nn(hot.astype(bf16), earlier)
    slot = jnp.sum(hot * ranks, axis=0, keepdims=True).astype(i32)
    which = consts[:, 0:1] ^ me
    turn = consts[:, 1:2]
    number = consts[:, 2:3]
    side = (iota((slots, both), 1) >= half).astype(i32)
    hit = (which == route) & (number == slot) & (turn == side)
    placer = hit.astype(f32).astype(bf16)
    place[...] = placer
    rows = nn(placer[:, 0:half], cot[...]) + nn(placer[:, half:both], cot_t[...])
    rows_out[...] = rows.astype(bf16)


def place_rows_body(idx, place, own, other, rows_out):
    half = own.shape[0]
    rows = nn(place[:, 0:half], own[...]) + nn(place[:, half : 2 * half], other[...])
    rows_out[...] = rows.astype(bf16)


def unplace_body(idx, place, rows, own, other):
    half = own.shape[0]
    arrived = rows[...]
    own[...] = tn(place[:, 0:half], arrived)
    other[...] = tn(place[:, half : 2 * half], arrived).astype(bf16)


def attend_body(
    experts, smalls, heads, idx,
    tokens, seg_c, seg_r, routes_c, wq, wk, wv, wo, s0, s1, hx, hy, da, db, tx, ty, ta, tb,
    w_all, small_all, q_o, k_o, v_o, probs_o, ctx_o, mixed_o, hcat_o, rp_o, *left,
):
    mine, core = idx[0], idx[2]
    rows, width = wq.shape
    length = tokens.shape[0]
    size = width // heads
    home = pl.multiple_of(mine * rows, 64)
    for m, w in enumerate((wq, wk, wv, wo)):
        w_all[m, pl.ds(home, rows), :] = w[...]
    for k, piece, held in ((1, hx, core), (2, hy, core), (1, tx, 1 - core), (2, ty, 1 - core)):
        at = pl.multiple_of((mine ^ k) * rows, 64)
        w_all[held, pl.ds(at, rows), :] = piece[0:rows, :]
        w_all[2 + held, pl.ds(at, rows), :] = piece[rows : 2 * rows, :]
    at = pl.multiple_of((mine ^ 3) * rows, 64)
    for first, second, held in ((da, db, core), (ta, tb, 1 - core)):
        w_all[held, pl.ds(at, rows), :] = first[0:rows, :]
        w_all[2 + held, pl.ds(at, rows), :] = second[...]
    small = jnp.zeros((smalls, width), f32)
    table_t = jnp.zeros((smalls, 128), f32)
    shard = 32 // 4
    for k, part in (
        (0, s0[...]), (1, s1[...]), (2, da[rows : rows + smalls, 0:256]), (3, da[rows : rows + smalls, 256:512])
    ):
        j = mine ^ k
        r, c = iota((256, width), 0), iota((256, width), 1)
        small = small + nn(part, ((r < rows) & (c == r + rows * j)).astype(f32).astype(bf16))
        r, c = iota((256, 128), 0), iota((256, 128), 1)
        keep = (r >= rows) & (r < rows + shard) & (c == r - rows + shard * j)
        table_t = table_t + nn(part, keep.astype(f32).astype(bf16))
    small_all[...] = small
    gain1 = small[experts : experts + 1, :]
    gain2 = small[experts + 1 : experts + 2, :]
    per_offset = nn(table_t.astype(bf16), bucket_onehot(128, length, False))

    x = tokens[...].astype(f32)
    h1 = (x * rms_scale(x) * gain1).astype(bf16)
    q_o[...] = nn(h1, w_all[0]).astype(bf16)
    k_o[...] = nn(h1, w_all[1]).astype(bf16)
    v_o[...] = nn(h1, w_all[2]).astype(bf16)
    same = seg_c[...] == seg_r[...]
    low = iota((length, 2 * size), 1) < size
    zero = jnp.zeros((length, 2 * size), bf16)
    for p in range(heads // 2):
        cols = slice(2 * size * p, 2 * size * (p + 1))
        q2, k2, v2 = q_o[:, cols], k_o[:, cols], v_o[:, cols]
        got = []
        for t in range(2):
            h = 2 * p + t
            qh = jnp.where(low, q2, zero) if t == 0 else jnp.where(low, zero, q2)
            line = per_offset[experts + 2 + h : experts + 3 + h, :]
            bias = pltpu.roll(
                jnp.broadcast_to(line, (length, 2 * length)), 0, 1, stride=1, stride_axis=0
            )[:, 0:length]
            s = jnp.where(same, nt(qh, k2) + bias, -1000000000.0)
            e = jnp.exp(s - jnp.max(s, axis=-1, keepdims=True))
            pr = e / jnp.sum(e, axis=-1, keepdims=True)
            probs_o[h] = pr
            got.append(nn(pr.astype(bf16), v2))
        ctx_o[:, cols] = jnp.where(low, got[0], got[1]).astype(bf16)
    mixed = x + nn(ctx_o[...], w_all[3])
    mixed_o[...] = mixed
    h2 = (mixed * rms_scale(mixed) * gain2).astype(bf16)
    logits = nt(h2, small[0:experts, :].astype(bf16))
    e = jnp.exp(logits - jnp.max(logits, axis=-1, keepdims=True))
    rp = e / jnp.sum(e, axis=-1, keepdims=True)
    rp_o[...] = rp
    hcat_o[...] = h2
    for zr, item in enumerate(left):

        @pl.when((idx[3] ^ zr) == owner_of[3])
        def _():
            item[...] = ctx_o[...]

        @pl.when((idx[3] ^ zr) != owner_of[3])
        def _():
            item[...] = tokens[...]


def back_in_body(idx, w_out, *refs):
    for k in range(4):
        refs[4][k] = nt(refs[k][...], w_out[...])


def expert_body(experts, idx, w_in, g_all, small_all, x0, x1, x2, x3, y0, y1, y2, y3, hid_o, dpre_o, gate_o):
    width = w_in.shape[0]
    slots = x0.shape[0]
    lane = iota((slots, 128), 1)
    wr_t = small_all[0:experts, :].astype(bf16)
    mine = iota((slots, experts), 1) == idx[1]
    for k, (x, y) in enumerate(((x0, y0), (x1, y1), (x2, y2), (x3, y3))):
        pre = nn(x[...], w_in[...])
        logits = nt(x[...], wr_t)
        e = jnp.exp(logits - jnp.max(logits, axis=-1, keepdims=True))
        gate = jnp.sum(jnp.where(mine, e, 0.0), axis=-1, keepdims=True) / jnp.sum(e, axis=-1, keepdims=True)
        gate_o[k] = jnp.broadcast_to(gate, (slots, 128))
        sq = pre * pre
        t = jnp.tanh(gelu_a * (pre + gelu_b * sq * pre))
        hid = (0.5 * pre * (1.0 + t)).astype(bf16)
        slope = 0.5 * (1.0 + t) + 0.5 * pre * (1.0 - t * t) * (gelu_a * (1.0 + 3.0 * gelu_b * sq))
        g = g_all[k]
        dpre = (gate * g * slope).astype(bf16)
        hid_o[k] = hid
        dpre_o[k] = dpre
        d_gate = jnp.sum(hid.astype(f32) * g, axis=-1, keepdims=True)
        y[:, 0:width] = nt(dpre, w_in[...]).astype(bf16)
        y[:, width : width + 128] = jnp.where(lane == 0, d_gate, 0.0).astype(bf16)


def expert_out_body(idx, w_out, hid, y0, y1, y2, y3):
    for k, y in enumerate((y0, y1, y2, y3)):
        y[...] = nn(hid[k], w_out[...]).astype(bf16)


def expert_grad_body(idx, hid, dpre, gate, x0, x1, x2, x3, g0, g1, g2, g3, gi, go):
    width = gi.shape[1]
    acc_i = jnp.zeros((width, dpre.shape[2]), f32)
    for k, x in enumerate((x0, x1, x2, x3)):
        acc_i = acc_i + tn(x[...], dpre[k])
    gi[0] = acc_i
    acc_o = jnp.zeros((hid.shape[2], width), f32)
    for k, g in enumerate((g0, g1, g2, g3)):
        acc_o = acc_o + tn(hid[k], (gate[k, :, 0:1] * g[...].astype(f32)).astype(bf16))
    go[0] = acc_o


def attend_back_body(
    experts, heads, chips, idx,
    own, other, mixed_r, cot, rp_r, routes_c, small_all, w_all, q, k, v, probs, ctx,
    dmixed_o, d_o, router_o, gain2_o, table_o, *rest,
):
    turned, diag = rest[:-1], rest[-1]
    length, width = mixed_r.shape
    size = width // heads
    back = own[...] + other[...].astype(f32)
    lane = iota((length, 128), 1)
    d_gate = jnp.sum(jnp.where(lane == 0, back[:, width : width + 128], 0.0), axis=-1, keepdims=True)
    hot = (routes_c[...] == iota((length, experts), 1)).astype(f32)
    rp = rp_r[...]
    gate = jnp.sum(rp * hot, axis=-1, keepdims=True)
    d_logits = (rp * (hot - gate) * d_gate).astype(bf16)
    gain2 = small_all[experts + 1 : experts + 2, :]
    wr_t = small_all[0:experts, :].astype(bf16)
    mixed = mixed_r[...]
    scale2 = rms_scale(mixed)
    normed2 = mixed * scale2
    h2 = (normed2 * gain2).astype(bf16)
    router_o[...] = tn(d_logits, h2)
    d_h2 = nn(d_logits, wr_t) + back[:, 0:width]
    gain2_o[...] = jnp.sum(d_h2 * normed2, axis=0, keepdims=True)
    d_mixed = cot[...].astype(f32) + norm_back(d_h2 * gain2, normed2, scale2)
    dmixed_o[...] = d_mixed
    d_attn = d_mixed.astype(bf16)
    d_o[3] = d_attn
    d_ctx = nt(d_attn, w_all[3]).astype(bf16)
    low = iota((length, 2 * size), 1) < size
    zero = jnp.zeros((length, 2 * size), bf16)
    blank = jnp.zeros((length, length), f32)
    upside = iota((length, length), 0) + iota((length, length), 1) == length - 1
    upside = upside.astype(f32).astype(bf16)
    for p in range(heads // 2):
        cols = slice(2 * size * p, 2 * size * (p + 1))
        q2, k2, v2, c2 = q[:, cols], k[:, cols], v[:, cols], d_ctx[:, cols]
        gq, gk, gv = [], [], []
        for t in range(2):
            h = 2 * p + t
            ch = jnp.where(low, c2, zero) if t == 0 else jnp.where(low, zero, c2)
            pr = probs[h]
            dw = nt(ch, v2)
            gv.append(tn(pr.astype(bf16), c2))
            ds = (pr * (dw - jnp.sum(pr * dw, axis=-1, keepdims=True))).astype(bf16)
            gq.append(nn(ds, k2))
            gk.append(tn(ds, q2))
            wide = jnp.concatenate([nn(upside, ds), blank], axis=1)
            wide = pltpu.roll(wide, 0, 1, stride=1, stride_axis=0)
            diag[h : h + 1, :] = jnp.sum(wide, axis=0, keepdims=True)
        d_o[0, :, cols] = jnp.where(low, gq[0], gq[1]).astype(bf16)
        d_o[1, :, cols] = jnp.where(low, gk[0], gk[1]).astype(bf16)
        d_o[2, :, cols] = jnp.where(low, gv[0], gv[1]).astype(bf16)
    sums = diag[0:heads, :]
    onehot = bucket_onehot(128, length, True)
    high = sums.astype(bf16)
    mid = (sums - high.astype(f32)).astype(bf16)
    table_o[...] = nt(high, onehot) + nt(mid, onehot)
    if chips == 4:
        z = idx[3]
        for zr in range(4):
            dest = z ^ zr
            for m in range(4):

                @pl.when(dest == owner_of[m])
                def _():
                    turned[zr][...] = d_o[m]


def token_grad_body(experts, smalls, idx, tokens, dmixed, d, w_all, small_all, router, gain2, table, dtok_o, small_o, table_o):
    x = tokens[...].astype(f32)
    scale1 = rms_scale(x)
    normed1 = x * scale1
    gain1 = small_all[experts : experts + 1, :]
    d_h1 = nt(d[0], w_all[0]) + nt(d[1], w_all[1]) + nt(d[2], w_all[2])
    g_gain1 = jnp.sum(d_h1 * normed1, axis=0, keepdims=True)
    dtok_o[...] = dmixed[...] + norm_back(d_h1 * gain1, normed1, scale1)
    width = x.shape[1]
    pick = (iota((smalls, experts), 0) == iota((smalls, experts), 1)).astype(f32).astype(bf16)
    line = iota((smalls, width), 0)
    out = nn(pick, router[...].astype(bf16))
    out = out + jnp.where(line == experts, g_gain1, 0.0) + jnp.where(line == experts + 1, gain2[...], 0.0)
    small_o[...] = out.astype(bf16)
    heads = table.shape[0]
    pick_t = (iota((smalls, heads), 0) == iota((smalls, heads), 1) + experts + 2).astype(f32)
    table_o[...] = nn(pick_t.astype(bf16), table[...].astype(bf16)).astype(bf16)


def mixer_grad_body(experts, idx, small_all, l0, l1, l2, l3, d0, d1, d2, d3, keep, send, acc, left):
    z, core = idx[3], idx[2]
    gain1 = small_all[experts : experts + 1, :]
    rows = l0.shape[0]

    @pl.when(z == owner_of[3])
    def _():
        for n, c in enumerate((l0, l1, l2, l3)):
            left[n * rows : (n + 1) * rows, :] = c[...]

    @pl.when(z != owner_of[3])
    def _():
        for n, item in enumerate((l0, l1, l2, l3)):
            x = item[...].astype(f32)
            left[n * rows : (n + 1) * rows, :] = (x * rms_scale(x) * gain1).astype(bf16)

    right = jnp.concatenate([d0[...], d1[...], d2[...], d3[...]], axis=0)
    acc[...] = tn(left[...], right)
    half = keep.shape[1]
    keep[...] = acc[:, pl.ds(pl.multiple_of(core * half, 128), half)]
    send[...] = acc[:, pl.ds(pl.multiple_of((1 - core) * half, 128), half)].astype(bf16)


def share_body(shard, idx, keep, got, small, table, s0, s1, s2, s3, total):
    mine = idx[0]
    total[...] = keep[...] + got[...].astype(f32)
    half = keep.shape[1]
    rows = total.shape[0] // 4
    width = small.shape[1]
    for k, out in enumerate((s0, s1, s2, s3)):
        j = mine ^ k
        out[0:rows, :] = total[pl.ds(pl.multiple_of(j * rows, 64), rows), :].astype(bf16)
        r, c = iota((width, half), 0), iota((width, half), 1)
        part = nn(small[...], ((c < rows) & (r == c + rows * j)).astype(f32).astype(bf16))
        r, c = iota((128, half), 0), iota((128, half), 1)
        keep_t = (c >= rows) & (c < rows + shard) & (r == c - rows + shard * j)
        part = part + nn(table[...], keep_t.astype(f32).astype(bf16))
        out[rows : rows + small.shape[0], :] = part.astype(bf16)


def sum_body(idx, a, b, c, d, out):
    out[...] = (
        a[...].astype(f32) + b[...].astype(f32) + c[...].astype(f32) + d[...].astype(f32)
    ).astype(bf16)


def finish_body(experts, idx, a0, a1, a2, a3, b0, b1, b2, b3, gq, gk, gv, go, router_t, gain_a, gain_b, tab):
    z, core = idx[3], idx[2]
    half = a0.shape[1]
    rows = gq.shape[0]
    at = pl.multiple_of(core * half, 128)
    off = pl.multiple_of((1 - core) * half, 128)
    for m, out in enumerate((gq, gk, gv, go)):
        for zr, (a, b) in enumerate(((a0, b0), (a1, b1), (a2, b2), (a3, b3))):

            @pl.when((z ^ zr) == owner_of[m])
            def _():
                out[:, pl.ds(at, half)] = a[0:rows, :].astype(f32)
                out[:, pl.ds(off, half)] = b[0:rows, :].astype(f32)

    total = jnp.zeros((a0.shape[0] - rows, half), f32)
    for item in (a0, a1, a2, a3, b0, b1, b2, b3):
        total = total + item[rows:, :].astype(f32)
    router_t[...] = total[0:experts, 0:rows]
    gain_a[...] = total[experts : experts + 1, 0:rows]
    gain_b[...] = total[experts + 1 : experts + 2, 0:rows]
    shard, heads = tab.shape
    lane = (iota((shard, half), 1) == iota((shard, half), 0) + rows).astype(f32)
    line = (iota((heads, total.shape[0]), 1) == iota((heads, total.shape[0]), 0) + experts + 2).astype(f32)
    dims = (((1,), (1,)), ((), ()))
    turned = lax.dot_general(lane, total, dims, precision=lax.Precision.HIGHEST, preferred_element_type=f32)
    tab[...] = lax.dot_general(turned, line, dims, precision=lax.Precision.HIGHEST, preferred_element_type=f32)


def on_device(
    tokens, w_query, w_key, w_value, w_attn_out, w_router, norm1_gain, norm2_gain, bias_table,
    w_expert_in, w_expert_out, routes, segments, cotangent,
):
    experts = lax.axis_size("expert")
    chips = experts // 2
    length, width = tokens.shape
    heads = bias_table.shape[1]
    rows = w_query.shape[0]
    shard = bias_table.shape[0]
    cap = 5 * length // (4 * experts)
    smalls = -(-(experts + 2 + heads) // 16) * 16
    slots = experts * cap
    wide = width + 128

    def along(x, axis, mask):
        n = lax.axis_size(axis)
        return lax.ppermute(x, axis, [(s, s ^ mask) for s in range(n)])

    def twin(x):
        return along(x, "expert", 1)

    def chip_exchange(x):
        cut = 2 * cap
        parts = [x[0:cut]]
        for zr in range(1, chips):
            parts.append(along(x[cut * zr : cut * (zr + 1)], "expert", 2 * zr))
        return jnp.concatenate(parts, axis=0)

    mine, me = lax.axis_index("dp"), lax.axis_index("expert")
    idx = jnp.stack([mine, me, me % 2, me // 2]).astype(i32)
    weight_in, weight_out = w_expert_in[0], w_expert_out[0]

    first = me % 2 == 0
    parcel = jnp.concatenate(
        [jnp.where(first, w_query, w_key), jnp.where(first, w_value, w_attn_out)], axis=0
    )
    hx = along(parcel, "dp", 1)
    hy = along(parcel, "dp", 2)

    wr_t, gain_a, gain_b, tab, cot, route_c, seg = lax.optimization_barrier(
        (w_router.T, norm1_gain, norm2_gain, bias_table, cotangent, routes, segments, parcel)
    )[:-1]
    small_own = call(
        "pack", 1, partial(pack_body, experts, smalls), [((smalls, 256), bf16)], idx,
        wr_t, gain_a[None], gain_b[None], tab,
    )[0]
    small_x = along(small_own, "dp", 1)
    route_row = route_c.reshape(1, length)
    routes2 = jnp.concatenate([route_row, twin(route_row.astype(f32)).astype(i32)], axis=1)
    r = np.arange(slots)
    consts = np.zeros((slots, 128), np.int32)
    consts[:, 0] = 2 * (r // (2 * cap))
    consts[:, 1] = (r // cap) % 2
    consts[:, 2] = r % cap
    place, g_rows = call(
        "place_cot", 1.5, partial(place_body, experts),
        [((slots, 2 * length), bf16), ((slots, width), bf16)], idx,
        jnp.asarray(consts), routes2, cot, twin(cot),
    )
    seg_c, seg_r = seg.reshape(length, 1), seg.reshape(1, length)
    g_here = chip_exchange(g_rows)
    hx, hy, place, g_here, seg_c, seg_r, route_c = lax.optimization_barrier(
        (hx, hy, place, g_here, seg_c, seg_r, route_c)
    )
    tail = jnp.zeros((smalls, width - 512), bf16)
    tail = jnp.concatenate([small_own, small_x, tail], axis=1)
    da = along(jnp.concatenate([hx[0:rows], tail], axis=0), "dp", 2)
    db = along(hy[rows:], "dp", 1)
    tx, ty = twin(hx), twin(hy)
    ta, tb = twin(da), twin(db)
    g_here = after(g_here, da, db)
    g_set = [g_here] + [along(g_here, "dp", k) for k in (1, 2, 3)]
    g_back = call("g_back", 2, back_in_body, [((4, slots, width), f32)], idx, weight_out, *g_set)[0]

    w_all, small_all, q, k, v, probs, ctx, mixed, hcat, rp, *left = call(
        "attend", 7, partial(attend_body, experts, smalls, heads),
        [
            ((4, width, width), bf16), ((smalls, width), f32),
            ((length, width), bf16), ((length, width), bf16), ((length, width), bf16),
            ((heads, length, length), f32), ((length, width), bf16), ((length, width), f32),
            ((length, width), bf16), ((length, experts), f32),
        ]
        + ([((length, width), bf16)] * 4 if chips == 4 else []),
        idx, tokens, seg_c, seg_r, route_c,
        w_query, w_key, w_value, w_attn_out, small_own, small_x, hx, hy, da, db, tx, ty, ta, tb,
    )

    x_rows = call("place_x", 1, place_rows_body, [((slots, width), bf16)], idx, place, hcat, twin(hcat))[0]
    x_here = chip_exchange(x_rows)
    x_set = [x_here] + [along(x_here, "dp", kk) for kk in (1, 2, 3)]
    if chips == 4:
        left = [left[0]] + [along(after(left[zr], x_here), "expert", 2 * zr) for zr in range(1, 4)]
        x_set[3] = after(x_set[3], left[1], left[2])
    *d_parts, hid, dpre, gates = call(
        "expert", 4, partial(expert_body, experts),
        [((slots, wide), bf16)] * 4 + [((4, slots, width), bf16)] * 2 + [((4, slots, 128), f32)],
        idx, weight_in, g_back, small_all, *x_set,
    )
    d_got = [d_parts[0]] + [along(d_parts[kk], "dp", kk) for kk in (1, 2, 3)]
    y_parts = call("expert_out", 1, expert_out_body, [((slots, width), bf16)] * 4, idx, weight_out, hid)
    grad_in, grad_out = call(
        "expert_grad", 5.5, expert_grad_body,
        [((1, width, weight_in.shape[1]), f32), ((1, weight_out.shape[0], width), f32)], idx,
        hid, dpre, gates, *x_set, *g_set,
    )
    d_here = call("sum_d", 0.7, sum_body, [((slots, wide), bf16)], idx, *d_got)[0]
    y_parts = list(lax.optimization_barrier((*y_parts, d_here))[:-1])
    y_got = [y_parts[0]] + [along(y_parts[kk], "dp", kk) for kk in (1, 2, 3)]
    d_rows = chip_exchange(d_here)
    place_d = after(place, *left) if chips == 4 else place
    back_own, back_other = call(
        "unplace_d", 1, unplace_body, [((length, wide), f32), ((length, wide), bf16)], idx, place_d, d_rows
    )
    back_other = twin(back_other)

    outs = [
        ((length, width), f32), ((4, length, width), bf16), ((experts, width), f32),
        ((1, width), f32), ((heads, 128), f32),
    ]
    if chips == 4:
        outs = outs + [((length, width), bf16)] * 4
    d_mixed, d_all, g_router, g_gain2, g_table, *turned = call(
        "attend_back", 5.5, partial(attend_back_body, experts, heads, chips), outs, idx,
        back_own, back_other, mixed, cotangent, rp, route_c, small_all, w_all, q, k, v, probs, ctx,
        scratch=[pltpu.VMEM((16, 2 * length), f32)],
    )
    d_in = [d_all]
    if chips == 4:
        d_in = [turned[0]] + [along(turned[zr], "expert", 2 * zr) for zr in range(1, 4)]
    d_tokens, small_g, table_g = call(
        "token_grad", 3, partial(token_grad_body, experts, smalls),
        [((length, width), f32), ((smalls, width), bf16), ((smalls, 128), bf16)], idx,
        tokens, d_mixed, d_all, w_all, small_all, g_router, g_gain2, g_table,
    )

    y_got[0] = after(y_got[0], d_mixed)
    y_here = call("sum_y", 0.7, sum_body, [((slots, width), bf16)], idx, *y_got)[0]
    if chips == 4:
        small_s, d_in[1] = lax.optimization_barrier((small_all, d_in[1], small_g, y_here))[0:2]
        keep, send = call(
            "mixer_grad", 2, partial(mixer_grad_body, experts),
            [((width, width // 2), f32), ((width, width // 2), bf16)], idx,
            small_s, *left, *d_in,
            scratch=[pltpu.VMEM((width, width), f32), pltpu.VMEM((4 * length, width), bf16)],
        )
        parts = call(
            "share", 1.2, partial(share_body, shard), [((rows + smalls, width // 2), bf16)] * 4, idx,
            keep, twin(send), small_g, table_g, scratch=[pltpu.VMEM((width, width // 2), f32)],
        )
        got = [parts[0]] + [along(parts[kk], "dp", kk) for kk in (1, 2, 3)]
        total = call("sum_share", 0.7, sum_body, [((rows + smalls, width // 2), bf16)], idx, *got)[0]
        y_here = after(y_here, got[2])
    y_rows = chip_exchange(y_here)
    y_own, y_other = call(
        "unplace_y", 1, unplace_body, [((length, width), f32), ((length, width), bf16)], idx, place, y_rows
    )
    y_other = twin(y_other)
    gate = jnp.sum(jnp.where(route_c == jnp.arange(experts, dtype=i32)[None, :], rp, 0.0), axis=1, keepdims=True)
    layer_out = (mixed + gate * (y_own + y_other.astype(f32))).astype(bf16)

    if chips == 4:
        a_set = [total] + [along(total, "expert", 2 * zr) for zr in range(1, 4)]
        b_set = [twin(a) for a in a_set]
        g_q, g_k, g_v, g_o, r_out, gain1_out, gain2_out, table_out = call(
            "finish", 2, partial(finish_body, experts),
            [((rows, width), f32)] * 4
            + [((experts, rows), f32), ((1, rows), f32), ((1, rows), f32), ((shard, heads), f32)],
            idx, *a_set, *b_set,
        )
        r_out, gain1_out, gain2_out = r_out.T, gain1_out[0], gain2_out[0]
    else:
        gain1 = small_all[experts : experts + 1]
        x = tokens.astype(f32)
        h1 = (x * rms_scale(x) * gain1).astype(bf16)
        both = jnp.concatenate(
            [tn(h1, d_all[0]), tn(h1, d_all[1]), tn(h1, d_all[2]), tn(ctx, d_all[3]), small_g.T.astype(f32)], axis=1
        )
        both = lax.psum_scatter(both, "dp", scatter_dimension=0, tiled=True)
        both = lax.psum(both, "expert")
        g_q, g_k, g_v, g_o = (both[:, m * width : (m + 1) * width] for m in range(4))
        rest = both[:, 4 * width :]
        r_out = rest[:, 0:experts]
        gain1_out, gain2_out = rest[:, experts], rest[:, experts + 1]
        tab_g = table_g.T[0 : 4 * shard, experts + 2 : experts + 2 + heads].astype(f32)
        table_out = lax.psum(lax.psum_scatter(tab_g, "dp", scatter_dimension=0, tiled=True), "expert")
    return (
        layer_out, d_tokens, g_q, g_k, g_v, g_o, r_out, gain1_out, gain2_out, table_out, grad_in, grad_out,
    )


def solution(mesh):
    return jax.shard_map(
        on_device,
        mesh=mesh,
        in_specs=(
            P(("dp", "expert"), None),
            P("dp", None),
            P("dp", None),
            P("dp", None),
            P("dp", None),
            P("dp", None),
            P("dp"),
            P("dp"),
            P("dp", None),
            P("expert", None, "dp"),
            P("expert", "dp", None),
            P(("dp", "expert"), None),
            P(("dp", "expert")),
            P(("dp", "expert"), None),
        ),
        out_specs=(
            P(("dp", "expert"), None),
            P(("dp", "expert"), None),
            P("dp", None),
            P("dp", None),
            P("dp", None),
            P("dp", None),
            P("dp", None),
            P("dp"),
            P("dp"),
            P("dp", None),
            P("expert", None, "dp"),
            P("expert", "dp", None),
        ),
        check_vma=False,
    )
```

```python
from functools import partial

import jax
import jax.numpy as jnp
import numpy as np
from jax import lax
from jax.experimental import pallas as pl
from jax.experimental.pallas import tpu as pltpu
from jax.sharding import PartitionSpec as P

eps = 1e-06
bucket_edges = (12, 16, 23, 32, 46, 64, 91)
f32 = jnp.float32
bf16 = jnp.bfloat16
i32 = jnp.int32
gelu_a = float(np.sqrt(2.0 / np.pi))
gelu_b = 0.044715

owner_of = (1, 2, 0, 3)


def nn(left, right):
    return lax.dot_general(left, right, (((1,), (0,)), ((), ())), preferred_element_type=f32)


def nt(left, right):
    return lax.dot_general(left, right, (((1,), (1,)), ((), ())), preferred_element_type=f32)


def tn(left, right):
    return lax.dot_general(left, right, (((0,), (0,)), ((), ())), preferred_element_type=f32)


def iota(shape, dim):
    return lax.broadcasted_iota(i32, shape, dim)


def after(value, *earlier):
    return lax.optimization_barrier((value, *earlier))[0]


def call(name, micros, body, outs, idx, *args, scratch=()):
    return pl.pallas_call(
        body,
        name=name,
        cost_estimate=pl.CostEstimate(flops=int(micros * 1.1e9), bytes_accessed=int(micros * 1e6), transcendentals=0),
        out_shape=[jax.ShapeDtypeStruct(s, d) for s, d in outs],
        in_specs=[pl.BlockSpec(memory_space=pltpu.SMEM)]
        + [pl.BlockSpec(memory_space=pltpu.VMEM)] * len(args),
        out_specs=[pl.BlockSpec(memory_space=pltpu.VMEM)] * len(outs),
        scratch_shapes=list(scratch),
        compiler_params=pltpu.CompilerParams(vmem_limit_bytes=40 * 1024 * 1024),
    )(idx, *args)


def rms_scale(values):
    return lax.rsqrt(jnp.mean(values * values, axis=-1, keepdims=True) + eps)


def norm_back(d_normed, normed, scale):
    return scale * (d_normed - normed * jnp.mean(d_normed * normed, axis=-1, keepdims=True))


def bucket_onehot(rows, length, centred):
    col = iota((rows, 2 * length), 1)
    n = (length - 1) - col if centred else jnp.where(col < length, -col, 2 * length - col)
    mag = jnp.abs(n)
    far = jnp.full_like(mag, 8)
    for threshold in bucket_edges:
        far = far + (mag >= threshold).astype(i32)
    bucket = jnp.where(n < 0, 16, 0) + jnp.where(mag < 8, mag, far)
    return (bucket == iota((rows, 2 * length), 0)).astype(f32).astype(bf16)


def pack_body(experts, smalls, idx, wr_t, g1, g2, tab, out):
    rows = wr_t.shape[1]
    heads, shard = tab.shape[1], tab.shape[0]
    pick = (iota((smalls, experts), 0) == iota((smalls, experts), 1)).astype(f32).astype(bf16)
    part = nn(pick, wr_t[...])
    line = iota((smalls, rows), 0)
    part = part + jnp.where(line == experts, g1[...].astype(f32), 0.0)
    part = part + jnp.where(line == experts + 1, g2[...].astype(f32), 0.0)
    width = out.shape[1]
    spread = (iota((rows, width), 0) == iota((rows, width), 1)).astype(f32).astype(bf16)
    whole = nn(part.astype(bf16), spread)
    pick_t = (iota((smalls, heads), 0) == iota((smalls, heads), 1)).astype(f32)
    table_t = nt(pick_t.astype(bf16), tab[...])
    spread_t = (iota((shard, width), 0) + rows == iota((shard, width), 1)).astype(f32)
    whole = whole + nn(table_t.astype(bf16), spread_t.astype(bf16))
    out[...] = whole.astype(bf16)


def place_body(experts, idx, consts, routes2, cot, cot_t, place, rows_out):
    me = idx[1]
    slots = place.shape[0]
    both = routes2.shape[1]
    half = both // 2
    route = routes2[...]
    hot = (iota((experts, both), 0) == route).astype(f32)
    a, b = iota((both, both), 0), iota((both, both), 1)
    earlier = ((a < b) & ((a < half) == (b < half))).astype(f32).astype(bf16)
    ranks = nn(hot.astype(bf16), earlier)
    slot = jnp.sum(hot * ranks, axis=0, keepdims=True).astype(i32)
    which = consts[:, 0:1] ^ me
    turn = consts[:, 1:2]
    number = consts[:, 2:3]
    side = (iota((slots, both), 1) >= half).astype(i32)
    hit = (which == route) & (number == slot) & (turn == side)
    placer = hit.astype(f32).astype(bf16)
    place[...] = placer
    rows = nn(placer[:, 0:half], cot[...]) + nn(placer[:, half:both], cot_t[...])
    rows_out[...] = rows.astype(bf16)


def place_rows_body(idx, place, own, other, rows_out):
    half = own.shape[0]
    rows = nn(place[:, 0:half], own[...]) + nn(place[:, half : 2 * half], other[...])
    rows_out[...] = rows.astype(bf16)


def unplace_body(idx, place, rows, own, other):
    half = own.shape[0]
    arrived = rows[...]
    own[...] = tn(place[:, 0:half], arrived)
    other[...] = tn(place[:, half : 2 * half], arrived).astype(bf16)


def attend_body(
    experts, smalls, heads, idx,
    tokens, seg_c, seg_r, routes_c, wq, wk, wv, wo, s0, s1, hx, hy, da, db, tx, ty, ta, tb,
    w_all, small_all, q_o, k_o, v_o, probs_o, ctx_o, mixed_o, hcat_o, rp_o, *left,
):
    mine, core = idx[0], idx[2]
    rows, width = wq.shape
    length = tokens.shape[0]
    size = width // heads
    home = pl.multiple_of(mine * rows, 64)
    for m, w in enumerate((wq, wk, wv, wo)):
        w_all[m, pl.ds(home, rows), :] = w[...]
    for k, piece, held in ((1, hx, core), (2, hy, core), (1, tx, 1 - core), (2, ty, 1 - core)):
        at = pl.multiple_of((mine ^ k) * rows, 64)
        w_all[held, pl.ds(at, rows), :] = piece[0:rows, :]
        w_all[2 + held, pl.ds(at, rows), :] = piece[rows : 2 * rows, :]
    at = pl.multiple_of((mine ^ 3) * rows, 64)
    for first, second, held in ((da, db, core), (ta, tb, 1 - core)):
        w_all[held, pl.ds(at, rows), :] = first[0:rows, :]
        w_all[2 + held, pl.ds(at, rows), :] = second[...]
    small = jnp.zeros((smalls, width), f32)
    table_t = jnp.zeros((smalls, 128), f32)
    shard = 32 // 4
    for k, part in (
        (0, s0[...]), (1, s1[...]), (2, da[rows : rows + smalls, 0:256]), (3, da[rows : rows + smalls, 256:512])
    ):
        j = mine ^ k
        r, c = iota((256, width), 0), iota((256, width), 1)
        small = small + nn(part, ((r < rows) & (c == r + rows * j)).astype(f32).astype(bf16))
        r, c = iota((256, 128), 0), iota((256, 128), 1)
        keep = (r >= rows) & (r < rows + shard) & (c == r - rows + shard * j)
        table_t = table_t + nn(part, keep.astype(f32).astype(bf16))
    small_all[...] = small
    gain1 = small[experts : experts + 1, :]
    gain2 = small[experts + 1 : experts + 2, :]
    per_offset = nn(table_t.astype(bf16), bucket_onehot(128, length, False))

    x = tokens[...].astype(f32)
    h1 = (x * rms_scale(x) * gain1).astype(bf16)
    q_o[...] = nn(h1, w_all[0]).astype(bf16)
    k_o[...] = nn(h1, w_all[1]).astype(bf16)
    v_o[...] = nn(h1, w_all[2]).astype(bf16)
    same = seg_c[...] == seg_r[...]
    low = iota((length, 2 * size), 1) < size
    zero = jnp.zeros((length, 2 * size), bf16)
    for p in range(heads // 2):
        cols = slice(2 * size * p, 2 * size * (p + 1))
        q2, k2, v2 = q_o[:, cols], k_o[:, cols], v_o[:, cols]
        got = []
        for t in range(2):
            h = 2 * p + t
            qh = jnp.where(low, q2, zero) if t == 0 else jnp.where(low, zero, q2)
            line = per_offset[h : h + 1, :]
            bias = pltpu.roll(
                jnp.broadcast_to(line, (length, 2 * length)), 0, 1, stride=1, stride_axis=0
            )[:, 0:length]
            s = jnp.where(same, nt(qh, k2) + bias, -1000000000.0)
            e = jnp.exp(s - jnp.max(s, axis=-1, keepdims=True))
            pr = e / jnp.sum(e, axis=-1, keepdims=True)
            probs_o[h] = pr
            got.append(nn(pr.astype(bf16), v2))
        ctx_o[:, cols] = jnp.where(low, got[0], got[1]).astype(bf16)
    mixed = x + nn(ctx_o[...], w_all[3])
    mixed_o[...] = mixed
    h2 = (mixed * rms_scale(mixed) * gain2).astype(bf16)
    logits = nt(h2, small[0:experts, :].astype(bf16))
    e = jnp.exp(logits - jnp.max(logits, axis=-1, keepdims=True))
    rp = e / jnp.sum(e, axis=-1, keepdims=True)
    rp_o[...] = rp
    hcat_o[...] = h2
    for zr, item in enumerate(left):

        @pl.when((idx[3] ^ zr) == owner_of[3])
        def _():
            item[...] = ctx_o[...]

        @pl.when((idx[3] ^ zr) != owner_of[3])
        def _():
            item[...] = tokens[...]


def back_in_body(idx, w_out, *refs):
    for k in range(4):
        refs[4][k] = nt(refs[k][...], w_out[...])


def expert_body(experts, idx, w_in, g_all, small_all, x0, x1, x2, x3, y0, y1, y2, y3, hid_o, dpre_o, gate_o):
    width = w_in.shape[0]
    slots = x0.shape[0]
    lane = iota((slots, 128), 1)
    wr_t = small_all[0:experts, :].astype(bf16)
    mine = iota((slots, experts), 1) == idx[1]
    for k, (x, y) in enumerate(((x0, y0), (x1, y1), (x2, y2), (x3, y3))):
        pre = nn(x[...], w_in[...])
        logits = nt(x[...], wr_t)
        e = jnp.exp(logits - jnp.max(logits, axis=-1, keepdims=True))
        gate = jnp.sum(jnp.where(mine, e, 0.0), axis=-1, keepdims=True) / jnp.sum(e, axis=-1, keepdims=True)
        gate_o[k] = jnp.broadcast_to(gate, (slots, 128))
        sq = pre * pre
        t = jnp.tanh(gelu_a * (pre + gelu_b * sq * pre))
        hid = (0.5 * pre * (1.0 + t)).astype(bf16)
        slope = 0.5 * (1.0 + t) + 0.5 * pre * (1.0 - t * t) * (gelu_a * (1.0 + 3.0 * gelu_b * sq))
        g = g_all[k]
        dpre = (gate * g * slope).astype(bf16)
        hid_o[k] = hid
        dpre_o[k] = dpre
        d_gate = jnp.sum(hid.astype(f32) * g, axis=-1, keepdims=True)
        y[:, 0:width] = nt(dpre, w_in[...]).astype(bf16)
        y[:, width : width + 128] = jnp.where(lane == 0, d_gate, 0.0).astype(bf16)


def expert_out_body(idx, w_out, hid, y0, y1, y2, y3):
    for k, y in enumerate((y0, y1, y2, y3)):
        y[...] = nn(hid[k], w_out[...]).astype(bf16)


def expert_grad_body(idx, hid, dpre, gate, x0, x1, x2, x3, g0, g1, g2, g3, gi, go):
    width = gi.shape[1]
    acc_i = jnp.zeros((width, dpre.shape[2]), f32)
    for k, x in enumerate((x0, x1, x2, x3)):
        acc_i = acc_i + tn(x[...], dpre[k])
    gi[0] = acc_i
    acc_o = jnp.zeros((hid.shape[2], width), f32)
    for k, g in enumerate((g0, g1, g2, g3)):
        acc_o = acc_o + tn(hid[k], (gate[k, :, 0:1] * g[...].astype(f32)).astype(bf16))
    go[0] = acc_o


def attend_back_body(
    experts, heads, chips, idx,
    own, other, mixed_r, cot, rp_r, routes_c, small_all, w_all, q, k, v, probs, ctx,
    dmixed_o, d_o, router_o, gain2_o, table_o, *rest,
):
    turned, diag = rest[:-1], rest[-1]
    length, width = mixed_r.shape
    size = width // heads
    back = own[...] + other[...].astype(f32)
    lane = iota((length, 128), 1)
    d_gate = jnp.sum(jnp.where(lane == 0, back[:, width : width + 128], 0.0), axis=-1, keepdims=True)
    hot = (routes_c[...] == iota((length, experts), 1)).astype(f32)
    rp = rp_r[...]
    gate = jnp.sum(rp * hot, axis=-1, keepdims=True)
    d_logits = (rp * (hot - gate) * d_gate).astype(bf16)
    gain2 = small_all[experts + 1 : experts + 2, :]
    wr_t = small_all[0:experts, :].astype(bf16)
    mixed = mixed_r[...]
    scale2 = rms_scale(mixed)
    normed2 = mixed * scale2
    h2 = (normed2 * gain2).astype(bf16)
    router_o[...] = tn(d_logits, h2)
    d_h2 = nn(d_logits, wr_t) + back[:, 0:width]
    gain2_o[...] = jnp.sum(d_h2 * normed2, axis=0, keepdims=True)
    d_mixed = cot[...].astype(f32) + norm_back(d_h2 * gain2, normed2, scale2)
    dmixed_o[...] = d_mixed
    d_attn = d_mixed.astype(bf16)
    d_o[3] = d_attn
    d_ctx = nt(d_attn, w_all[3]).astype(bf16)
    low = iota((length, 2 * size), 1) < size
    zero = jnp.zeros((length, 2 * size), bf16)
    blank = jnp.zeros((length, length), f32)
    upside = iota((length, length), 0) + iota((length, length), 1) == length - 1
    upside = upside.astype(f32).astype(bf16)
    for p in range(heads // 2):
        cols = slice(2 * size * p, 2 * size * (p + 1))
        q2, k2, v2, c2 = q[:, cols], k[:, cols], v[:, cols], d_ctx[:, cols]
        gq, gk, gv = [], [], []
        for t in range(2):
            h = 2 * p + t
            ch = jnp.where(low, c2, zero) if t == 0 else jnp.where(low, zero, c2)
            pr = probs[h]
            dw = nt(ch, v2)
            gv.append(tn(pr.astype(bf16), c2))
            ds = (pr * (dw - jnp.sum(pr * dw, axis=-1, keepdims=True))).astype(bf16)
            gq.append(nn(ds, k2))
            gk.append(tn(ds, q2))
            wide = jnp.concatenate([nn(upside, ds), blank], axis=1)
            wide = pltpu.roll(wide, 0, 1, stride=1, stride_axis=0)
            diag[h : h + 1, :] = jnp.sum(wide, axis=0, keepdims=True)
        d_o[0, :, cols] = jnp.where(low, gq[0], gq[1]).astype(bf16)
        d_o[1, :, cols] = jnp.where(low, gk[0], gk[1]).astype(bf16)
        d_o[2, :, cols] = jnp.where(low, gv[0], gv[1]).astype(bf16)
    sums = diag[0:heads, :]
    onehot = bucket_onehot(128, length, True)
    high = sums.astype(bf16)
    mid = (sums - high.astype(f32)).astype(bf16)
    table_o[...] = nt(high, onehot) + nt(mid, onehot)
    if chips == 4:
        z = idx[3]
        for zr in range(4):
            dest = z ^ zr
            for m in range(4):

                @pl.when(dest == owner_of[m])
                def _():
                    turned[zr][...] = d_o[m]


def token_grad_body(experts, smalls, idx, tokens, dmixed, d, w_all, small_all, router, gain2, table, dtok_o, small_o, table_o):
    x = tokens[...].astype(f32)
    scale1 = rms_scale(x)
    normed1 = x * scale1
    gain1 = small_all[experts : experts + 1, :]
    d_h1 = nt(d[0], w_all[0]) + nt(d[1], w_all[1]) + nt(d[2], w_all[2])
    g_gain1 = jnp.sum(d_h1 * normed1, axis=0, keepdims=True)
    dtok_o[...] = dmixed[...] + norm_back(d_h1 * gain1, normed1, scale1)
    width = x.shape[1]
    pick = (iota((smalls, experts), 0) == iota((smalls, experts), 1)).astype(f32).astype(bf16)
    line = iota((smalls, width), 0)
    out = nn(pick, router[...].astype(bf16))
    out = out + jnp.where(line == experts, g_gain1, 0.0) + jnp.where(line == experts + 1, gain2[...], 0.0)
    small_o[...] = out.astype(bf16)
    heads = table.shape[0]
    pick_t = (iota((smalls, heads), 0) == iota((smalls, heads), 1)).astype(f32)
    table_o[...] = nn(pick_t.astype(bf16), table[...].astype(bf16)).astype(bf16)


def mixer_grad_body(experts, idx, small_all, l0, l1, l2, l3, d0, d1, d2, d3, keep, send, acc, left):
    z, core = idx[3], idx[2]
    gain1 = small_all[experts : experts + 1, :]
    rows = l0.shape[0]

    @pl.when(z == owner_of[3])
    def _():
        for n, c in enumerate((l0, l1, l2, l3)):
            left[n * rows : (n + 1) * rows, :] = c[...]

    @pl.when(z != owner_of[3])
    def _():
        for n, item in enumerate((l0, l1, l2, l3)):
            x = item[...].astype(f32)
            left[n * rows : (n + 1) * rows, :] = (x * rms_scale(x) * gain1).astype(bf16)

    right = jnp.concatenate([d0[...], d1[...], d2[...], d3[...]], axis=0)
    acc[...] = tn(left[...], right)
    half = keep.shape[1]
    keep[...] = acc[:, pl.ds(pl.multiple_of(core * half, 128), half)]
    send[...] = acc[:, pl.ds(pl.multiple_of((1 - core) * half, 128), half)].astype(bf16)


def share_body(shard, idx, keep, got, small, table, s0, s1, s2, s3, total):
    mine = idx[0]
    total[...] = keep[...] + got[...].astype(f32)
    half = keep.shape[1]
    rows = total.shape[0] // 4
    width = small.shape[1]
    for k, out in enumerate((s0, s1, s2, s3)):
        j = mine ^ k
        out[0:rows, :] = total[pl.ds(pl.multiple_of(j * rows, 64), rows), :].astype(bf16)
        r, c = iota((width, half), 0), iota((width, half), 1)
        part = nn(small[...], ((c < rows) & (r == c + rows * j)).astype(f32).astype(bf16))
        r, c = iota((128, half), 0), iota((128, half), 1)
        keep_t = (c >= rows) & (c < rows + shard) & (r == c - rows + shard * j)
        part = part + nn(table[...], keep_t.astype(f32).astype(bf16))
        out[rows : rows + small.shape[0], :] = part.astype(bf16)


def sum_body(idx, a, b, c, d, out):
    out[...] = (
        a[...].astype(f32) + b[...].astype(f32) + c[...].astype(f32) + d[...].astype(f32)
    ).astype(bf16)


def finish_body(experts, idx, a0, a1, a2, a3, b0, b1, b2, b3, gq, gk, gv, go, router_t, gain_a, gain_b, tab):
    z, core = idx[3], idx[2]
    half = a0.shape[1]
    rows = gq.shape[0]
    at = pl.multiple_of(core * half, 128)
    off = pl.multiple_of((1 - core) * half, 128)
    for m, out in enumerate((gq, gk, gv, go)):
        for zr, (a, b) in enumerate(((a0, b0), (a1, b1), (a2, b2), (a3, b3))):

            @pl.when((z ^ zr) == owner_of[m])
            def _():
                out[:, pl.ds(at, half)] = a[0:rows, :].astype(f32)
                out[:, pl.ds(off, half)] = b[0:rows, :].astype(f32)

    total = jnp.zeros((a0.shape[0] - rows, half), f32)
    for item in (a0, a1, a2, a3, b0, b1, b2, b3):
        total = total + item[rows:, :].astype(f32)
    router_t[...] = total[0:experts, 0:rows]
    gain_a[...] = total[experts : experts + 1, 0:rows]
    gain_b[...] = total[experts + 1 : experts + 2, 0:rows]
    shard, heads = tab.shape
    lane = (iota((shard, half), 1) == iota((shard, half), 0) + rows).astype(f32)
    line = (iota((heads, total.shape[0]), 1) == iota((heads, total.shape[0]), 0)).astype(f32)
    dims = (((1,), (1,)), ((), ()))
    turned = lax.dot_general(lane, total, dims, precision=lax.Precision.HIGHEST, preferred_element_type=f32)
    tab[...] = lax.dot_general(turned, line, dims, precision=lax.Precision.HIGHEST, preferred_element_type=f32)


def on_device(
    tokens, w_query, w_key, w_value, w_attn_out, w_router, norm1_gain, norm2_gain, bias_table,
    w_expert_in, w_expert_out, routes, segments, cotangent,
):
    experts = lax.axis_size("expert")
    chips = experts // 2
    length, width = tokens.shape
    heads = bias_table.shape[1]
    rows = w_query.shape[0]
    shard = bias_table.shape[0]
    cap = 5 * length // (4 * experts)
    smalls = -(-max(experts + 2, heads) // 16) * 16
    slots = experts * cap
    wide = width + 128

    def along(x, axis, mask):
        n = lax.axis_size(axis)
        return lax.ppermute(x, axis, [(s, s ^ mask) for s in range(n)])

    def twin(x):
        return along(x, "expert", 1)

    def chip_exchange(x):
        cut = 2 * cap
        parts = [x[0:cut]]
        for zr in range(1, chips):
            parts.append(along(x[cut * zr : cut * (zr + 1)], "expert", 2 * zr))
        return jnp.concatenate(parts, axis=0)

    mine, me = lax.axis_index("dp"), lax.axis_index("expert")
    idx = jnp.stack([mine, me, me % 2, me // 2]).astype(i32)
    weight_in, weight_out = w_expert_in[0], w_expert_out[0]

    first = me % 2 == 0
    parcel = jnp.concatenate(
        [jnp.where(first, w_query, w_key), jnp.where(first, w_value, w_attn_out)], axis=0
    )
    hx = along(parcel, "dp", 1)
    hy = along(parcel, "dp", 2)

    wr_t, gain_a, gain_b, tab, cot, route_c, seg = lax.optimization_barrier(
        (w_router.T, norm1_gain, norm2_gain, bias_table, cotangent, routes, segments, parcel)
    )[:-1]
    small_own = call(
        "pack", 1, partial(pack_body, experts, smalls), [((smalls, 256), bf16)], idx,
        wr_t, gain_a[None], gain_b[None], tab,
    )[0]
    small_x = along(small_own, "dp", 1)
    route_row = route_c.reshape(1, length)
    routes2 = jnp.concatenate([route_row, twin(route_row.astype(f32)).astype(i32)], axis=1)
    r = np.arange(slots)
    consts = np.zeros((slots, 128), np.int32)
    consts[:, 0] = 2 * (r // (2 * cap))
    consts[:, 1] = (r // cap) % 2
    consts[:, 2] = r % cap
    place, g_rows = call(
        "place_cot", 1.5, partial(place_body, experts),
        [((slots, 2 * length), bf16), ((slots, width), bf16)], idx,
        jnp.asarray(consts), routes2, cot, twin(cot),
    )
    seg_c, seg_r = seg.reshape(length, 1), seg.reshape(1, length)
    g_here = chip_exchange(g_rows)
    hx, hy, place, g_here, seg_c, seg_r, route_c = lax.optimization_barrier(
        (hx, hy, place, g_here, seg_c, seg_r, route_c)
    )
    tail = jnp.zeros((smalls, width - 512), bf16)
    tail = jnp.concatenate([small_own, small_x, tail], axis=1)
    da = along(jnp.concatenate([hx[0:rows], tail], axis=0), "dp", 2)
    db = along(hy[rows:], "dp", 1)
    tx, ty = twin(hx), twin(hy)
    ta, tb = twin(da), twin(db)
    g_here = after(g_here, da, db)
    g_set = [g_here] + [along(g_here, "dp", k) for k in (1, 2, 3)]
    g_back = call("g_back", 2, back_in_body, [((4, slots, width), f32)], idx, weight_out, *g_set)[0]

    w_all, small_all, q, k, v, probs, ctx, mixed, hcat, rp, *left = call(
        "attend", 7, partial(attend_body, experts, smalls, heads),
        [
            ((4, width, width), bf16), ((smalls, width), f32),
            ((length, width), bf16), ((length, width), bf16), ((length, width), bf16),
            ((heads, length, length), f32), ((length, width), bf16), ((length, width), f32),
            ((length, width), bf16), ((length, experts), f32),
        ]
        + ([((length, width), bf16)] * 4 if chips == 4 else []),
        idx, tokens, seg_c, seg_r, route_c,
        w_query, w_key, w_value, w_attn_out, small_own, small_x, hx, hy, da, db, tx, ty, ta, tb,
    )

    x_rows = call("place_x", 1, place_rows_body, [((slots, width), bf16)], idx, place, hcat, twin(hcat))[0]
    x_here = chip_exchange(x_rows)
    x_set = [x_here] + [along(x_here, "dp", kk) for kk in (1, 2, 3)]
    if chips == 4:
        left = [left[0]] + [along(after(left[zr], x_here), "expert", 2 * zr) for zr in range(1, 4)]
        x_set[3] = after(x_set[3], left[1], left[2])
    *d_parts, hid, dpre, gates = call(
        "expert", 4, partial(expert_body, experts),
        [((slots, wide), bf16)] * 4 + [((4, slots, width), bf16)] * 2 + [((4, slots, 128), f32)],
        idx, weight_in, g_back, small_all, *x_set,
    )
    d_got = [d_parts[0]] + [along(d_parts[kk], "dp", kk) for kk in (1, 2, 3)]
    y_parts = call("expert_out", 1, expert_out_body, [((slots, width), bf16)] * 4, idx, weight_out, hid)
    grad_in, grad_out = call(
        "expert_grad", 5.5, expert_grad_body,
        [((1, width, weight_in.shape[1]), f32), ((1, weight_out.shape[0], width), f32)], idx,
        hid, dpre, gates, *x_set, *g_set,
    )
    d_here = call("sum_d", 0.7, sum_body, [((slots, wide), bf16)], idx, *d_got)[0]
    y_parts = list(lax.optimization_barrier((*y_parts, d_here))[:-1])
    y_got = [y_parts[0]] + [along(y_parts[kk], "dp", kk) for kk in (1, 2, 3)]
    d_rows = chip_exchange(d_here)
    place_d = after(place, *left) if chips == 4 else place
    back_own, back_other = call(
        "unplace_d", 1, unplace_body, [((length, wide), f32), ((length, wide), bf16)], idx, place_d, d_rows
    )
    back_other = twin(back_other)

    outs = [
        ((length, width), f32), ((4, length, width), bf16), ((experts, width), f32),
        ((1, width), f32), ((heads, 128), f32),
    ]
    if chips == 4:
        outs = outs + [((length, width), bf16)] * 4
    d_mixed, d_all, g_router, g_gain2, g_table, *turned = call(
        "attend_back", 5.5, partial(attend_back_body, experts, heads, chips), outs, idx,
        back_own, back_other, mixed, cotangent, rp, route_c, small_all, w_all, q, k, v, probs, ctx,
        scratch=[pltpu.VMEM((16, 2 * length), f32)],
    )
    d_in = [d_all]
    if chips == 4:
        d_in = [turned[0]] + [along(turned[zr], "expert", 2 * zr) for zr in range(1, 4)]
    d_tokens, small_g, table_g = call(
        "token_grad", 3, partial(token_grad_body, experts, smalls),
        [((length, width), f32), ((smalls, width), bf16), ((smalls, 128), bf16)], idx,
        tokens, d_mixed, d_all, w_all, small_all, g_router, g_gain2, g_table,
    )

    y_got[0] = after(y_got[0], d_mixed)
    y_here = call("sum_y", 0.7, sum_body, [((slots, width), bf16)], idx, *y_got)[0]
    if chips == 4:
        small_s, d_in[1] = lax.optimization_barrier((small_all, d_in[1], small_g, y_here))[0:2]
        keep, send = call(
            "mixer_grad", 2, partial(mixer_grad_body, experts),
            [((width, width // 2), f32), ((width, width // 2), bf16)], idx,
            small_s, *left, *d_in,
            scratch=[pltpu.VMEM((width, width), f32), pltpu.VMEM((4 * length, width), bf16)],
        )
        parts = call(
            "share", 1.2, partial(share_body, shard), [((rows + smalls, width // 2), bf16)] * 4, idx,
            keep, twin(send), small_g, table_g, scratch=[pltpu.VMEM((width, width // 2), f32)],
        )
        got = [parts[0]] + [along(parts[kk], "dp", kk) for kk in (1, 2, 3)]
        total = call("sum_share", 0.7, sum_body, [((rows + smalls, width // 2), bf16)], idx, *got)[0]
        y_here = after(y_here, got[2])
    y_rows = chip_exchange(y_here)
    y_own, y_other = call(
        "unplace_y", 1, unplace_body, [((length, width), f32), ((length, width), bf16)], idx, place, y_rows
    )
    y_other = twin(y_other)
    gate = jnp.sum(jnp.where(route_c == jnp.arange(experts, dtype=i32)[None, :], rp, 0.0), axis=1, keepdims=True)
    layer_out = (mixed + gate * (y_own + y_other.astype(f32))).astype(bf16)

    if chips == 4:
        a_set = [total] + [along(total, "expert", 2 * zr) for zr in range(1, 4)]
        b_set = [twin(a) for a in a_set]
        g_q, g_k, g_v, g_o, r_out, gain1_out, gain2_out, table_out = call(
            "finish", 2, partial(finish_body, experts),
            [((rows, width), f32)] * 4
            + [((experts, rows), f32), ((1, rows), f32), ((1, rows), f32), ((shard, heads), f32)],
            idx, *a_set, *b_set,
        )
        r_out, gain1_out, gain2_out = r_out.T, gain1_out[0], gain2_out[0]
    else:
        gain1 = small_all[experts : experts + 1]
        x = tokens.astype(f32)
        h1 = (x * rms_scale(x) * gain1).astype(bf16)
        both = jnp.concatenate(
            [tn(h1, d_all[0]), tn(h1, d_all[1]), tn(h1, d_all[2]), tn(ctx, d_all[3]), small_g.T.astype(f32)], axis=1
        )
        both = lax.psum_scatter(both, "dp", scatter_dimension=0, tiled=True)
        both = lax.psum(both, "expert")
        g_q, g_k, g_v, g_o = (both[:, m * width : (m + 1) * width] for m in range(4))
        rest = both[:, 4 * width :]
        r_out = rest[:, 0:experts]
        gain1_out, gain2_out = rest[:, experts], rest[:, experts + 1]
        tab_g = table_g.T[0 : 4 * shard, 0:heads].astype(f32)
        table_out = lax.psum(lax.psum_scatter(tab_g, "dp", scatter_dimension=0, tiled=True), "expert")
    return (
        layer_out, d_tokens, g_q, g_k, g_v, g_o, r_out, gain1_out, gain2_out, table_out, grad_in, grad_out,
    )


def solution(mesh):
    return jax.shard_map(
        on_device,
        mesh=mesh,
        in_specs=(
            P(("dp", "expert"), None),
            P("dp", None),
            P("dp", None),
            P("dp", None),
            P("dp", None),
            P("dp", None),
            P("dp"),
            P("dp"),
            P("dp", None),
            P("expert", None, "dp"),
            P("expert", "dp", None),
            P(("dp", "expert"), None),
            P(("dp", "expert")),
            P(("dp", "expert"), None),
        ),
        out_specs=(
            P(("dp", "expert"), None),
            P(("dp", "expert"), None),
            P("dp", None),
            P("dp", None),
            P("dp", None),
            P("dp", None),
            P("dp", None),
            P("dp"),
            P("dp"),
            P("dp", None),
            P("expert", None, "dp"),
            P("expert", "dp", None),
        ),
        check_vma=False,
    )
```
